32 devices in a mesh: parts: 2 (over x), seg: 2 (over core), sec: 8 (over z, y).
Axes of the slice: x: 2, y: 2, z: 4, core: 2. Of those that a mesh axis runs over, the one named last changes fastest.
Arguments:
- initial_state: bfloat16 [4, 16, 128, 128], P(('parts', 'seg'), 'sec'), parts along dimension 0, may hold values from -6 to 6
- left_blocks: bfloat16 [4, 16, 24, 128, 128], P(('parts', 'seg'), 'sec'), parts along dimension 0, may hold values from -2 to 3
- right_blocks: bfloat16 [4, 16, 24, 128, 128], P(('parts', 'seg'), 'sec'), parts along dimension 0, may hold values from -2 to 3
- sources: int32 [4, 16, 32], P(('parts', 'seg'), 'sec'), parts along dimension 0, may hold values from 0 to 15, as said below
- channels: int32 [4, 16, 32], P(('parts', 'seg'), 'sec'), parts along dimension 0, may hold values from 0 to 23
- couplings: float32 [4, 16, 32], P(('parts', 'seg'), 'sec'), parts along dimension 0, may hold values from -1 to 6
- kept_rank: int32 [4, 16], P(('parts', 'seg'), 'sec'), parts along dimension 0, may hold values from 32 to 128
Outputs:
- kept_state: bfloat16 [4, 16, 128, 128], P(('parts', 'seg'), 'sec'), parts along dimension 0
- energies: float32 [4, 3], P(('parts', 'seg')), parts along dimension 0
The draws below stay inside these ranges and needn't reach their ends.
There are 2 independent parts, one for each index of `parts`. The reference program is written for one: setup_inputs(seed, part) draws one part's arguments, and reference() takes and returns one part's arrays. A program takes and returns all parts, laid end to end along the dimension named above; each array names one. Nothing has to cross between parts.
Inputs may be any that keep to these rules, and one draw needn't show every extreme that they name: `sources`: pair 0 of block t has source t. Block t keeps its first kept_rank columns.
All inputs are finite; a program needn't handle non-finite values.
Results may differ from the reference program's by a relative error of at most 0.017.
Values may be sent and summed in bfloat16 or wider, within the bound.
No kernel may reach another device: no remote copies, remote signals or barrier semaphores. Data moves between devices by JAX's collectives and lax.ppermute only.
A program may use at most 64 MiB of HBM per device.

```python
import math
import jax
import jax.numpy as jnp
from jax import lax

B = 128
W = 24
K = 32
ITERS = 3
N_SEG_ALL = 2
NSEC = 16
ENTRIES = 262144


def first_pair():
    return jnp.arange(K, dtype=jnp.int32)[None, None, :] == 0


def onsite_identity():
    diagonal_cells = jnp.arange(B, dtype=jnp.int32)[:, None] == jnp.arange(B, dtype=jnp.int32)[None, :]
    first_channel = jnp.arange(W, dtype=jnp.int32)[:, None, None] == 0
    return (diagonal_cells[None, :, :] & first_channel).astype(jnp.float32)


def draw_sources(key, part):
    key = jax.random.fold_in(key, 101)
    drawn = jax.random.randint(key, (N_SEG_ALL, NSEC, K), 0, NSEC, dtype=jnp.int32)
    own_block = jnp.broadcast_to(jnp.arange(NSEC, dtype=jnp.int32)[None, :, None], (N_SEG_ALL, NSEC, K))
    return jnp.where(first_pair(), own_block, drawn)


def draw_channels(key, part):
    key = jax.random.fold_in(key, 103)
    drawn = jax.random.randint(key, (N_SEG_ALL, NSEC, K), 0, W, dtype=jnp.int32)
    return jnp.where(first_pair(), jnp.int32(0), drawn)


def draw_couplings(key, part):
    key = jax.random.fold_in(key, 105)
    key_rest, key_level, key_factor = jax.random.split(key, 3)
    shape = (N_SEG_ALL, NSEC, K)
    rest = jnp.clip(0.18 * jax.random.normal(key_rest, shape, jnp.float32), -1.0, 1.0)
    level = jax.random.uniform(key_level, (N_SEG_ALL, 1, 1), jnp.float32, 0.3, 1.0)
    factor = jnp.exp(jax.random.uniform(key_factor, (N_SEG_ALL, NSEC, 1), jnp.float32, math.log(0.5), math.log(1.5)))
    ramp = 1.0 + 2.0 * jnp.arange(NSEC, dtype=jnp.float32)[None, :, None] / max(NSEC - 1, 1)
    onsite = level * ramp * factor
    return jnp.where(first_pair(), onsite, rest)


def draw_left_blocks(key, part):
    key = jax.random.fold_in(key, 107)
    shape = (N_SEG_ALL, NSEC, W, B, B)
    noise = jax.random.normal(key, shape, jnp.float32) / math.sqrt(B)
    return (noise + onsite_identity()).astype(jnp.bfloat16)


def draw_right_blocks(key, part):
    key = jax.random.fold_in(key, 109)
    shape = (N_SEG_ALL, NSEC, W, B, B)
    noise = jax.random.normal(key, shape, jnp.float32) / math.sqrt(B)
    return (noise + onsite_identity()).astype(jnp.bfloat16)


def with_ends(result, key, low, high):
    place = [jax.random.randint(jax.random.fold_in(key, axis), (), 0, length) for axis, length in enumerate(result.shape)]
    widest = result.shape.index(max(result.shape))
    next_to = place[:widest] + [(place[widest] + 1) % result.shape[widest]] + place[widest + 1:]
    return result.at[tuple(place)].set(low).at[tuple(next_to)].set(high)


def block_scale(own_key, dims, pieces, least, largest):
    def one(position, shards_of):
        draws = jax.random.uniform(jax.random.fold_in(jax.random.fold_in(own_key, 6), position), (shards_of,), jnp.float32, least / len(pieces), largest / len(pieces))
        return jnp.repeat(jnp.exp(draws), dims[position] // shards_of).reshape((-1,) + (1,) * (len(dims) - position - 1))

    level = one(*pieces[0])
    for cut in pieces[1:]:
        level = level * one(*cut)
    return level


def bell_draw(stream_key, shape, width, limit, cuts=(), kind=jnp.bfloat16):
    values = jax.random.normal(stream_key, shape, jnp.float32) * width
    if len(cuts) > 0:
        values = block_scale(stream_key, shape, cuts, -0.22, 0.18) * values
    return jnp.clip(values, min=-limit, max=limit).astype(kind)


def setup_inputs(seed: int = 0, part: int = 0) -> dict:
    key_list = jax.random.split(jax.random.key(seed), 8)
    own_keys = jax.random.split(jax.random.fold_in(key_list[7], part), 8)
    initial_state = bell_draw(own_keys[0], (N_SEG_ALL, NSEC, B, B), 1.0, 6.0, ((0, 2), (1, 8)))
    left_blocks = draw_left_blocks(jax.random.fold_in(jax.random.fold_in(key_list[7], part), 71), part)
    right_blocks = draw_right_blocks(jax.random.fold_in(jax.random.fold_in(key_list[7], part), 71), part)
    sources = draw_sources(jax.random.fold_in(jax.random.fold_in(key_list[7], part), 71), part)
    channels = draw_channels(jax.random.fold_in(jax.random.fold_in(key_list[7], part), 71), part)
    couplings = draw_couplings(jax.random.fold_in(jax.random.fold_in(key_list[7], part), 71), part)
    kept_rank = with_ends(jax.random.randint(own_keys[6], (N_SEG_ALL, NSEC), B // 4, B + 1), jax.random.fold_in(own_keys[6], 1), B // 4, B).astype(jnp.int32)
    return {"initial_state": initial_state, "left_blocks": left_blocks, "right_blocks": right_blocks, "sources": sources, "channels": channels, "couplings": couplings, "kept_rank": kept_rank}


step_length = 0.5
epsilon = 1e-06

def coefficient_table(sources, channels, couplings):
    sector_ids = jnp.arange(NSEC, dtype=jnp.int32)
    channel_ids = jnp.arange(W, dtype=jnp.int32)
    one_source = (sources[..., None] == sector_ids).astype(jnp.float32)
    one_channel = (channels[..., None] == channel_ids).astype(jnp.float32) * couplings[..., None]
    return jnp.einsum('gtkw,gtks->gtws', one_channel, one_source, precision=lax.Precision.HIGHEST)

def hamiltonian_image(current, coefficients, left_blocks, right_used):
    segments = current.shape[0]
    flattened = current.reshape(segments, NSEC, B * B)
    mixture = jnp.einsum('gtws,gsx->gtwx', coefficients, flattened, precision=lax.Precision.HIGHEST)
    mixture = lax.optimization_barrier(mixture.reshape(segments, NSEC, W, B, B).astype(jnp.bfloat16)).astype(jnp.float32)
    partial_value = jnp.einsum('gtwij,gtwjk->gtwik', left_blocks.astype(jnp.float32), mixture)
    partial_value = lax.optimization_barrier(partial_value.astype(jnp.bfloat16)).astype(jnp.float32)
    image = jnp.einsum('gtwik,gtwlk->gtil', partial_value, right_used.astype(jnp.float32))
    return image.astype(jnp.bfloat16)

def reference(initial_state, left_blocks, right_blocks, sources, channels, couplings, kept_rank):
    coefficients = coefficient_table(sources, channels, couplings)
    right_used = jnp.flip(right_blocks, axis=0)
    current = initial_state.astype(jnp.float32)
    energy_list = []
    for iteration in range(ITERS):
        image = hamiltonian_image(current, coefficients, left_blocks, right_used).astype(jnp.float32)
        intersection = lax.optimization_barrier(jnp.sum(current * image, axis=(1, 2, 3)))
        squares = lax.optimization_barrier(jnp.sum(current * current, axis=(1, 2, 3)))
        energy = intersection / squares
        current = (1.0 + step_length * energy)[:, None, None, None] * current - step_length * image
        energy_list.append(energy)
    column_ids = jnp.arange(B, dtype=jnp.int32)
    keep_mask = column_ids[None, None, None, :] < kept_rank[:, :, None, None]
    truncated = jnp.where(keep_mask, current, jnp.float32(0.0))
    kept_sq = lax.optimization_barrier(jnp.sum(truncated * truncated, axis=(1, 2, 3)))
    kept_state = (truncated / jnp.sqrt(kept_sq / ENTRIES + epsilon)[:, None, None, None]).astype(jnp.bfloat16)
    return (kept_state, jnp.stack(energy_list, axis=1))
```

```python
import functools

import jax
import jax.numpy as jnp
from jax import lax
from jax.experimental import pallas as pl
from jax.experimental.pallas import tpu as pltpu
from jax.sharding import PartitionSpec as P

ITERS = 3
STEP = 0.5
EPSILON = 1e-06
SMEM = pl.BlockSpec(memory_space=pltpu.SMEM)
VMEM = pl.BlockSpec(memory_space=pltpu.VMEM)
NEAR = (0, 1, 2, 4, 6, 3, 5, 7)


def hop(block, distance):
    count = lax.axis_size("sec")
    return lax.ppermute(block, "sec", [(a, a ^ distance) for a in range(count)])


def gather(block):
    if lax.axis_size("sec") != len(NEAR):
        return [lax.all_gather(block, "sec", axis=0, tiled=True)]
    return [block] + [hop(block, distance) for distance in NEAR[1:]]


def slots(sector, local_count):
    if lax.axis_size("sec") != len(NEAR):
        return sector
    place = sorted(range(len(NEAR)), key=lambda position: NEAR[position])
    apart = (sector // local_count) ^ lax.axis_index("sec")
    found = sum(jnp.where(apart == d, place[d], 0) for d in range(len(NEAR)))
    return found * local_count + sector % local_count


def pair_table(sources, channels, couplings, local_count):
    k = jnp.arange(sources.shape[1], dtype=jnp.int32)
    before = (channels[:, None, :] < channels[:, :, None]) | (
        (channels[:, None, :] == channels[:, :, None]) & (k[None, None, :] < k[None, :, None])
    )
    rank = jnp.sum(before.astype(jnp.int32), axis=2)
    chosen = rank[:, None, :] == k[None, :, None]

    def ordered(values):
        return jnp.sum(jnp.where(chosen, values[:, None, :], jnp.zeros((), values.dtype)), axis=2)

    channel = ordered(channels)
    same = jnp.concatenate(
        [jnp.zeros_like(channel[:, :1]), (channel[:, 1:] == channel[:, :-1]).astype(jnp.int32)], axis=1
    )
    ints = jnp.stack([ordered(slots(sources, local_count)), channel, same], axis=1)
    return ints, ordered(couplings)


def apply_operator(ints, floats, state, left, right, mixed, image):
    blocks, width = left.shape[0], left.shape[1]
    pairs = floats.shape[1]
    mixed[...] = jnp.zeros_like(mixed)
    for t in range(blocks):
        total = jnp.zeros(state.shape[1:], jnp.float32)
        for k in range(pairs):
            term = floats[t, k] * state[ints[t, 0, k]]
            total = term + jnp.where(ints[t, 2, k] == 1, total, 0.0)
            mixed[t, ints[t, 1, k]] = total.astype(jnp.bfloat16)
    for t in range(blocks):
        result = jnp.zeros(image.shape[1:], jnp.float32)
        for w in range(0, width, 2):
            halves = [
                jnp.dot(left[t, v], mixed[t, v], preferred_element_type=jnp.float32).astype(jnp.bfloat16)
                for v in (w, w + 1)
            ]
            result += lax.dot_general(
                jnp.concatenate(halves, axis=1),
                jnp.concatenate([right[t, w], right[t, w + 1]], axis=1),
                (((1,), (1,)), ((), ())),
                preferred_element_type=jnp.float32,
            )
        image[t] = result.astype(jnp.bfloat16)


def spread(pieces, target):
    at = 0
    for piece in pieces:
        size = piece.shape[0]
        target[at : at + size] = piece[...].astype(jnp.float32)
        at += size


def first_kernel(count, ints, floats, left, right, *refs):
    pieces, (image, state, mixed) = refs[:count], refs[count:]
    spread(pieces, state)
    apply_operator(ints, floats, state, left, right, mixed, image)


def rayleigh_update(before, images, after):
    shape = before[0].shape[1:]
    intersection = jnp.zeros(shape, jnp.float32)
    squares = jnp.zeros(shape, jnp.float32)
    at = 0
    flat = []
    for piece in before:
        flat += [(piece, s) for s in range(piece.shape[0])]
    pictures = []
    for piece in images:
        pictures += [(piece, s) for s in range(piece.shape[0])]
    for (piece, s), (picture, p) in zip(flat, pictures):
        value = piece[s].astype(jnp.float32)
        intersection += value * picture[p].astype(jnp.float32)
        squares += value * value
    energy = jnp.sum(intersection) / jnp.sum(squares)
    growth = 1.0 + STEP * energy
    for (piece, s), (picture, p) in zip(flat, pictures):
        after[at] = growth * piece[s].astype(jnp.float32) - STEP * picture[p].astype(jnp.float32)
        at += 1
    return energy


def middle_kernel(states, count, ints, floats, left, right, *refs):
    before, images = refs[:states], refs[states : states + count]
    energy, state, image, mixed = refs[states + count :]
    energy[0, 0] = rayleigh_update(before, images, state)
    apply_operator(ints, floats, state, left, right, mixed, image)


def last_kernel(states, count, ints, floats, ranks, left, right, *refs):
    before, images = refs[:states], refs[states : states + count]
    energy, own, image, sums, state, mixed = refs[states + count :]
    energy[0, 0] = rayleigh_update(before, images, state)
    apply_operator(ints, floats, state, left, right, mixed, image)
    blocks, size = image.shape[0], image.shape[1]
    own[...] = state[:blocks]
    intersection = jnp.zeros((size, size), jnp.float32)
    squares = jnp.zeros((size, size), jnp.float32)
    for t in range(blocks):
        value = own[t]
        intersection += value * image[t].astype(jnp.float32)
        squares += value * value
    intersection, squares = jnp.sum(intersection), jnp.sum(squares)
    here = jnp.where(squares > 1e-30, intersection / jnp.maximum(squares, 1e-30), 0.0)
    growth = 1.0 + STEP * here
    column = lax.broadcasted_iota(jnp.int32, (size, size), 1)
    dd = jnp.zeros((size, size), jnp.float32)
    dc = jnp.zeros((size, size), jnp.float32)
    cc = jnp.zeros((size, size), jnp.float32)
    for t in range(blocks):
        keep = column < ranks[t]
        value = jnp.where(keep, own[t], 0.0)
        moved = growth * value - STEP * jnp.where(keep, image[t].astype(jnp.float32), 0.0)
        dd += moved * moved
        dc += moved * value
        cc += value * value
    row = lax.broadcasted_iota(jnp.int32, sums.shape, 1)
    result = jnp.zeros(sums.shape, jnp.float32)
    for at, number in enumerate([intersection, squares, here, jnp.sum(dd), jnp.sum(dc), jnp.sum(cc)]):
        result = jnp.where(row == at, number, result)
    sums[...] = result


def finish_kernel(count, entries, ranks, own, image, *refs):
    gathered, (energy, kept) = refs[:count], refs[count:]
    rows = []
    for piece in gathered:
        rows += [piece[s] for s in range(piece.shape[0])]
    intersection = sum(row[0:1, :] for row in rows)
    squares = sum(row[1:2, :] for row in rows)
    total = intersection / squares
    kept_sq = jnp.zeros_like(total)
    for row in rows:
        shift = STEP * (total - row[2:3, :])
        kept_sq += row[3:4, :] + 2.0 * shift * row[4:5, :] + shift * shift * row[5:6, :]
    energy[...] = jnp.broadcast_to(total, energy.shape)
    growth = 1.0 + STEP * total
    scale = 1.0 / jnp.sqrt(jnp.maximum(kept_sq, 0.0) / entries + EPSILON)
    size = image.shape[1]
    column = lax.broadcasted_iota(jnp.int32, (size, size), 1)
    for t in range(image.shape[0]):
        value = growth * own[t] - STEP * image[t].astype(jnp.float32)
        kept[t] = (jnp.where(column < ranks[t], value, 0.0) * scale).astype(jnp.bfloat16)


def local(initial_state, left_blocks, right_blocks, sources, channels, couplings, kept_rank):
    start = initial_state[0]
    left = left_blocks[0]
    right = lax.ppermute(right_blocks[0], "seg", [(0, 1), (1, 0)])
    blocks, size = start.shape[0], start.shape[1]
    width = left.shape[1]
    sectors = blocks * lax.axis_size("sec")
    entries = float(sectors * size * size)
    ranks = kept_rank[0]
    ints, floats = pair_table(sources[0], channels[0], couplings[0], blocks)

    own_type = jax.ShapeDtypeStruct((blocks, size, size), jnp.bfloat16)
    number = jax.ShapeDtypeStruct((1, 1), jnp.float32)
    whole = (sectors, size, size)
    mixed = pltpu.VMEM((blocks, width, size, size), jnp.bfloat16)
    params = pltpu.CompilerParams(vmem_limit_bytes=24 * 2**20)

    states = gather(start)
    image = pl.pallas_call(
        functools.partial(first_kernel, len(states)),
        out_shape=own_type,
        in_specs=[SMEM, SMEM] + [VMEM] * (2 + len(states)),
        out_specs=VMEM,
        scratch_shapes=[pltpu.VMEM(whole, jnp.float32), mixed],
        compiler_params=params,
        name="first_image",
    )(ints, floats, left, right, *states)
    energies = []
    for iteration in range(1, ITERS - 1):
        images = gather(image)
        energy, state, image = pl.pallas_call(
            functools.partial(middle_kernel, len(states), len(images)),
            out_shape=(number, jax.ShapeDtypeStruct(whole, jnp.float32), own_type),
            in_specs=[SMEM, SMEM] + [VMEM] * (2 + len(states) + len(images)),
            out_specs=(SMEM, VMEM, VMEM),
            scratch_shapes=[mixed],
            compiler_params=params,
            name="middle_image",
        )(ints, floats, left, right, *states, *images)
        states = [state]
        energies.append(energy)
    images = gather(image)
    energy, own, image, sums = pl.pallas_call(
        functools.partial(last_kernel, len(states), len(images)),
        out_shape=(
            number,
            jax.ShapeDtypeStruct((blocks, size, size), jnp.float32),
            own_type,
            jax.ShapeDtypeStruct((1, 8, 128), jnp.float32),
        ),
        in_specs=[SMEM, SMEM, SMEM] + [VMEM] * (2 + len(states) + len(images)),
        out_specs=(SMEM, VMEM, VMEM, VMEM),
        scratch_shapes=[pltpu.VMEM(whole, jnp.float32), mixed],
        compiler_params=params,
        name="last_image",
    )(ints, floats, ranks, left, right, *states, *images)
    energies.append(energy)
    gathered = gather(sums)
    energy, kept = pl.pallas_call(
        functools.partial(finish_kernel, len(gathered), entries),
        out_shape=(jax.ShapeDtypeStruct((1, 128), jnp.float32), own_type),
        in_specs=[SMEM] + [VMEM] * (2 + len(gathered)),
        out_specs=(VMEM, VMEM),
        compiler_params=params,
        name="finish",
    )(ranks, own, image, *gathered)
    energies.append(energy[:, :1])
    return kept[None], jnp.concatenate(energies, axis=1)


def solution(mesh):
    return jax.shard_map(
        local,
        mesh=mesh,
        in_specs=(
            P(("parts", "seg"), "sec", None, None),
            P(("parts", "seg"), "sec", None, None, None),
            P(("parts", "seg"), "sec", None, None, None),
            P(("parts", "seg"), "sec", None),
            P(("parts", "seg"), "sec", None),
            P(("parts", "seg"), "sec", None),
            P(("parts", "seg"), "sec"),
        ),
        out_specs=(P(("parts", "seg"), "sec", None, None), P(("parts", "seg"), None)),
        check_vma=False,
    )
```

```python
import functools

import jax
import jax.numpy as jnp
from jax import lax
from jax.experimental import pallas as pl
from jax.experimental.pallas import tpu as pltpu
from jax.sharding import PartitionSpec as P

ITERS = 3
STEP = 0.5
EPSILON = 1e-06
SMEM = pl.BlockSpec(memory_space=pltpu.SMEM)
VMEM = pl.BlockSpec(memory_space=pltpu.VMEM)
ANY = pl.BlockSpec(memory_space=pl.ANY)
APART = (0, 4, 3, 7, 2, 6, 1, 5)


def hop(block, distance):
    count = lax.axis_size("sec")
    return lax.ppermute(block, "sec", [(a, a ^ distance) for a in range(count)])


def gather(block):
    if lax.axis_size("sec") != len(APART):
        return [lax.all_gather(block, "sec", axis=0, tiled=True)]
    both = jnp.concatenate([block, hop(block, 4)])
    return [both] + [hop(both, distance) for distance in (3, 2, 1)]


def slot(sector, blocks, devices, here):
    if devices != len(APART):
        return sector
    apart = lax.div(sector, blocks) ^ here
    place = jnp.int32(0)
    for position in range(1, devices):
        place = jnp.where(apart == APART[position], position, place)
    return place * blocks + lax.rem(sector, blocks)


def table_kernel(width, devices, here, sources, channels, couplings, ints, floats, starts):
    blocks, pairs = sources.shape
    for t in range(blocks):

        def clear(w, carry):
            starts[w] = 0
            return carry

        def count(k, carry):
            starts[channels[t, k] + 1] += 1
            return carry

        def add(w, total):
            total += starts[w]
            starts[w] = total
            return total

        def put(k, carry):
            channel = channels[t, k]
            to = starts[channel]
            starts[channel] = to + 1
            ints[t, 0, to] = slot(sources[t, k], blocks, devices, here[0])
            ints[t, 1, to] = channel
            floats[t, to] = couplings[t, k]
            return carry

        def compare(k, carry):
            ints[t, 2, k] = (ints[t, 1, k] == ints[t, 1, k - 1]).astype(jnp.int32)
            return carry

        lax.fori_loop(0, width + 1, clear, 0)
        lax.fori_loop(0, pairs, count, 0)
        lax.fori_loop(0, width + 1, add, jnp.int32(0))
        lax.fori_loop(0, pairs, put, 0)
        ints[t, 2, 0] = 0
        lax.fori_loop(1, pairs, compare, 0)


def fetch(sources, targets, semaphores):
    copies = [
        pltpu.make_async_copy(source, target, semaphores.at[at])
        for at, (source, target) in enumerate(zip(sources, targets))
    ]
    for copy in copies:
        copy.start()
    return copies


def apply_operator(ints, floats, state, copies, left, right, mixed, image):
    blocks, width = left.shape[0], left.shape[1]
    pairs = floats.shape[1]
    mixed[...] = jnp.zeros_like(mixed)
    for t in range(blocks):
        total = jnp.zeros(state.shape[1:], jnp.float32)
        for k in range(pairs):
            term = floats[t, k] * state[ints[t, 0, k]]
            total = term + jnp.where(ints[t, 2, k] == 1, total, 0.0)
            mixed[t, ints[t, 1, k]] = total.astype(jnp.bfloat16)
    for copy in copies:
        copy.wait()
    for t in range(blocks):
        result = jnp.zeros(image.shape[1:], jnp.float32)
        for w in range(0, width, 2):
            halves = [
                jnp.dot(left[t, v], mixed[t, v], preferred_element_type=jnp.float32).astype(jnp.bfloat16)
                for v in (w, w + 1)
            ]
            result += lax.dot_general(
                jnp.concatenate(halves, axis=1),
                jnp.concatenate([right[t, w], right[t, w + 1]], axis=1),
                (((1,), (1,)), ((), ())),
                preferred_element_type=jnp.float32,
            )
        image[t] = result.astype(jnp.bfloat16)


def spread(pieces, target):
    at = 0
    for piece in pieces:
        size = piece.shape[0]
        target[at : at + size] = piece[...].astype(jnp.float32)
        at += size


def first_kernel(count, ints, floats, *refs):
    environment, pieces, (image, state, mixed, left, right, semaphores) = refs[:2], refs[2 : 2 + count], refs[2 + count :]
    copies = fetch(environment, (left, right), semaphores)
    spread(pieces, state)
    apply_operator(ints, floats, state, copies, left, right, mixed, image)


def rayleigh_update(before, images, after):
    shape = before[0].shape[1:]
    intersection = jnp.zeros(shape, jnp.float32)
    squares = jnp.zeros(shape, jnp.float32)
    at = 0
    flat = []
    for piece in before:
        flat += [(piece, s) for s in range(piece.shape[0])]
    pictures = []
    for piece in images:
        pictures += [(piece, s) for s in range(piece.shape[0])]
    for (piece, s), (picture, p) in zip(flat, pictures):
        value = piece[s].astype(jnp.float32)
        intersection += value * picture[p].astype(jnp.float32)
        squares += value * value
    energy = jnp.sum(intersection) / jnp.sum(squares)
    growth = 1.0 + STEP * energy
    for (piece, s), (picture, p) in zip(flat, pictures):
        after[at] = growth * piece[s].astype(jnp.float32) - STEP * picture[p].astype(jnp.float32)
        at += 1
    return energy


def middle_kernel(states, count, ints, floats, *refs):
    environment, before, images = refs[:2], refs[2 : 2 + states], refs[2 + states : 2 + states + count]
    energy, state, image, mixed, left, right, semaphores = refs[2 + states + count :]
    copies = fetch(environment, (left, right), semaphores)
    energy[...] = jnp.full(energy.shape, rayleigh_update(before, images, state))
    apply_operator(ints, floats, state, copies, left, right, mixed, image)


def last_kernel(states, count, ints, floats, ranks, *refs):
    environment, before, images = refs[:2], refs[2 : 2 + states], refs[2 + states : 2 + states + count]
    energy, own, image, sums, state, mixed, left, right, semaphores = refs[2 + states + count :]
    copies = fetch(environment, (left, right), semaphores)
    energy[...] = jnp.full(energy.shape, rayleigh_update(before, images, state))
    apply_operator(ints, floats, state, copies, left, right, mixed, image)
    blocks, size = image.shape[0], image.shape[1]
    own[...] = state[:blocks]
    intersection = jnp.zeros((size, size), jnp.float32)
    squares = jnp.zeros((size, size), jnp.float32)
    for t in range(blocks):
        value = own[t]
        intersection += value * image[t].astype(jnp.float32)
        squares += value * value
    intersection, squares = jnp.sum(intersection), jnp.sum(squares)
    here = jnp.where(squares > 1e-30, intersection / jnp.maximum(squares, 1e-30), 0.0)
    growth = 1.0 + STEP * here
    column = lax.broadcasted_iota(jnp.int32, (size, size), 1)
    dd = jnp.zeros((size, size), jnp.float32)
    dc = jnp.zeros((size, size), jnp.float32)
    cc = jnp.zeros((size, size), jnp.float32)
    for t in range(blocks):
        keep = column < ranks[t]
        value = jnp.where(keep, own[t], 0.0)
        moved = growth * value - STEP * jnp.where(keep, image[t].astype(jnp.float32), 0.0)
        dd += moved * moved
        dc += moved * value
        cc += value * value
    row = lax.broadcasted_iota(jnp.int32, sums.shape, 1)
    result = jnp.zeros(sums.shape, jnp.float32)
    for at, number in enumerate([intersection, squares, here, jnp.sum(dd), jnp.sum(dc), jnp.sum(cc)]):
        result = jnp.where(row == at, number, result)
    sums[...] = result


def finish_kernel(steps, count, entries, ranks, own, image, *refs):
    earlier, gathered, (energies, kept) = refs[:steps], refs[steps : steps + count], refs[steps + count :]
    rows = []
    for piece in gathered:
        rows += [piece[s] for s in range(piece.shape[0])]
    intersection = sum(row[0:1, :] for row in rows)
    squares = sum(row[1:2, :] for row in rows)
    total = intersection / squares
    kept_sq = jnp.zeros_like(total)
    for row in rows:
        shift = STEP * (total - row[2:3, :])
        kept_sq += row[3:4, :] + 2.0 * shift * row[4:5, :] + shift * shift * row[5:6, :]
    column = lax.broadcasted_iota(jnp.int32, total.shape, 1)
    listed = total
    for step, energy in enumerate(earlier):
        listed = jnp.where(column == step, energy[...], listed)
    energies[...] = listed[:, : steps + 1]
    growth = 1.0 + STEP * total
    scale = 1.0 / jnp.sqrt(jnp.maximum(kept_sq, 0.0) / entries + EPSILON)
    size = image.shape[1]
    column = lax.broadcasted_iota(jnp.int32, (size, size), 1)
    for t in range(image.shape[0]):
        value = growth * own[t] - STEP * image[t].astype(jnp.float32)
        kept[t] = (jnp.where(column < ranks[t], value, 0.0) * scale).astype(jnp.bfloat16)


def local(initial_state, left_blocks, right_blocks, sources, channels, couplings, kept_rank):
    start = initial_state[0]
    left = left_blocks[0]
    right = lax.ppermute(right_blocks[0], "seg", [(0, 1), (1, 0)])
    blocks, size = start.shape[0], start.shape[1]
    width = left.shape[1]
    sectors = blocks * lax.axis_size("sec")
    entries = float(sectors * size * size)
    ranks = kept_rank[0]
    devices = lax.axis_size("sec")
    pairs = sources.shape[2]
    params = pltpu.CompilerParams(vmem_limit_bytes=32 * 2**20)
    ints, floats = pl.pallas_call(
        functools.partial(table_kernel, width, devices),
        out_shape=(
            jax.ShapeDtypeStruct((blocks, 3, pairs), jnp.int32),
            jax.ShapeDtypeStruct((blocks, pairs), jnp.float32),
        ),
        in_specs=[SMEM] * 4,
        out_specs=(SMEM, SMEM),
        scratch_shapes=[pltpu.SMEM((width + 1,), jnp.int32)],
        compiler_params=params,
        name="pair_table",
    )(lax.axis_index("sec").reshape(1), sources[0], channels[0], couplings[0])

    own_type = jax.ShapeDtypeStruct((blocks, size, size), jnp.bfloat16)
    number = jax.ShapeDtypeStruct((1, 128), jnp.float32)
    whole = (sectors, size, size)
    scratch = [
        pltpu.VMEM(left.shape, jnp.bfloat16),
        pltpu.VMEM(left.shape, jnp.bfloat16),
        pltpu.VMEM(left.shape, jnp.bfloat16),
        pltpu.SemaphoreType.DMA((2,)),
    ]

    states = gather(start)
    image = pl.pallas_call(
        functools.partial(first_kernel, len(states)),
        out_shape=own_type,
        in_specs=[SMEM, SMEM, ANY, ANY] + [VMEM] * len(states),
        out_specs=VMEM,
        scratch_shapes=[pltpu.VMEM(whole, jnp.float32)] + scratch,
        compiler_params=params,
        name="first_image",
    )(ints, floats, left, right, *states)
    energies = []
    for _ in range(1, ITERS - 1):
        images = gather(image)
        energy, state, image = pl.pallas_call(
            functools.partial(middle_kernel, len(states), len(images)),
            out_shape=(number, jax.ShapeDtypeStruct(whole, jnp.float32), own_type),
            in_specs=[SMEM, SMEM, ANY, ANY] + [VMEM] * (len(states) + len(images)),
            out_specs=(VMEM, VMEM, VMEM),
            scratch_shapes=scratch,
            compiler_params=params,
            name="middle_image",
        )(ints, floats, left, right, *states, *images)
        states = [state]
        energies.append(energy)
    images = gather(image)
    energy, own, image, sums = pl.pallas_call(
        functools.partial(last_kernel, len(states), len(images)),
        out_shape=(
            number,
            jax.ShapeDtypeStruct((blocks, size, size), jnp.float32),
            own_type,
            jax.ShapeDtypeStruct((1, 8, 128), jnp.float32),
        ),
        in_specs=[SMEM, SMEM, SMEM, ANY, ANY] + [VMEM] * (len(states) + len(images)),
        out_specs=(VMEM, VMEM, VMEM, VMEM),
        scratch_shapes=[pltpu.VMEM(whole, jnp.float32)] + scratch,
        compiler_params=params,
        name="last_image",
    )(ints, floats, ranks, left, right, *states, *images)
    energies.append(energy)
    gathered = gather(sums)
    energies, kept = pl.pallas_call(
        functools.partial(finish_kernel, len(energies), len(gathered), entries),
        out_shape=(jax.ShapeDtypeStruct((1, ITERS), jnp.float32), own_type),
        in_specs=[SMEM] + [VMEM] * (2 + len(energies) + len(gathered)),
        out_specs=(VMEM, VMEM),
        compiler_params=params,
        name="finish",
    )(ranks, own, image, *energies, *gathered)
    return kept[None], energies


def solution(mesh):
    return jax.shard_map(
        local,
        mesh=mesh,
        in_specs=(
            P(("parts", "seg"), "sec", None, None),
            P(("parts", "seg"), "sec", None, None, None),
            P(("parts", "seg"), "sec", None, None, None),
            P(("parts", "seg"), "sec", None),
            P(("parts", "seg"), "sec", None),
            P(("parts", "seg"), "sec", None),
            P(("parts", "seg"), "sec"),
        ),
        out_specs=(P(("parts", "seg"), "sec", None, None), P(("parts", "seg"), None)),
        check_vma=False,
    )
```

```python
import functools

import jax
import jax.numpy as jnp
from jax import lax
from jax.experimental import pallas as pl
from jax.experimental.pallas import tpu as pltpu
from jax.sharding import PartitionSpec as P

ITERS = 3
STEP = 0.5
EPSILON = 1e-06
SMEM = pl.BlockSpec(memory_space=pltpu.SMEM)
VMEM = pl.BlockSpec(memory_space=pltpu.VMEM)
ANY = pl.BlockSpec(memory_space=pl.ANY)
HBM = pl.BlockSpec(memory_space=pltpu.HBM)
APART = (0, 4, 1, 2, 3, 7, 6, 5)


def hop(block, distance):
    count = lax.axis_size("sec")
    return lax.ppermute(block, "sec", [(a, a ^ distance) for a in range(count)])


def gather(block):
    if lax.axis_size("sec") != len(APART):
        return [lax.all_gather(block, "sec", axis=0, tiled=True)]
    relayed = hop(block, 4)
    near = [hop(block, distance) for distance in (1, 2, 3)]
    return [block, relayed] + near + [hop(relayed, distance) for distance in (3, 2, 1)]


def gather_small(block):
    if lax.axis_size("sec") != len(APART):
        return [lax.all_gather(block, "sec", axis=0, tiled=True)]
    line = jnp.concatenate([block] + [hop(block, distance) for distance in (2, 4, 6)])
    return [line, hop(line, 1)]


def slot(sector, blocks, devices, here):
    if devices != len(APART):
        return sector
    apart = lax.div(sector, blocks) ^ here
    place = jnp.int32(0)
    for position in range(1, devices):
        place = jnp.where(apart == APART[position], position, place)
    return place * blocks + lax.rem(sector, blocks)


def prepare_kernel(devices, *refs):
    arguments, left, (codes, floats, near), scratch = refs[:3], refs[3], refs[4:7], refs[7:]
    sources, channels, couplings, starts, semaphores = scratch
    copies = fetch((*arguments, left), (sources, channels, couplings, near), semaphores)
    blocks, pairs = sources.shape
    width = near.shape[1]
    here = lax.axis_index("sec")
    seen = 1 << 16
    for w in range(width + 1):
        for t in range(blocks):
            starts[t, w] = 0
    for copy in copies[:3]:
        copy.wait()

    def count(k, carry):
        for t in range(blocks):
            starts[t, channels[t, k] + 1] += 1
        return carry

    def add(w, totals):
        totals = tuple(totals[t] + starts[t, w] for t in range(blocks))
        for t in range(blocks):
            starts[t, w] = totals[t]
        return totals

    def put(k, carry):
        for t in range(blocks):
            channel = channels[t, k]
            mark = starts[t, channel]
            to = mark & (seen - 1)
            starts[t, channel] = (to + 1) | seen
            same = lax.shift_right_logical(mark, 16)
            code = slot(sources[t, k], blocks, devices, here)
            codes[t, to] = (code << 16) | (channel << 1) | same
            floats[t, to] = couplings[t, k]
        return carry

    lax.fori_loop(0, pairs, count, 0, unroll=4)
    lax.fori_loop(0, width + 1, add, (jnp.int32(0),) * blocks, unroll=5)
    lax.fori_loop(0, pairs, put, 0, unroll=2)
    copies[3].wait()


def fetch(sources, targets, semaphores):
    copies = [
        pltpu.make_async_copy(source, target, semaphores.at[at])
        for at, (source, target) in enumerate(zip(sources, targets))
    ]
    for copy in copies:
        copy.start()
    return copies


def apply_operator(copies, codes, floats, state, left, right, mixed, image):
    blocks, width = left.shape[0], left.shape[1]
    pairs = floats.shape[1]
    for t in range(blocks):
        mixed[t][...] = jnp.zeros_like(mixed[t])
    for copy in copies:
        copy.wait()
    for t in range(blocks):
        total = jnp.zeros(state.shape[1:], jnp.float32)
        for k in range(pairs):
            code = codes[t, k]
            term = floats[t, k] * state[lax.shift_right_logical(code, 16)]
            total = term + jnp.where((code & 1) == 1, total, 0.0)
            mixed[t][lax.shift_right_logical(code, 1) & 0x7FFF] = total.astype(jnp.bfloat16)
    for t in range(blocks):
        result = jnp.zeros(image.shape[1:], jnp.float32)
        for w in range(0, width, 2):
            halves = [
                jnp.dot(left[t, v], mixed[t][v], preferred_element_type=jnp.float32).astype(jnp.bfloat16)
                for v in (w, w + 1)
            ]
            result += lax.dot_general(
                jnp.concatenate(halves, axis=1),
                jnp.concatenate([right[t, w], right[t, w + 1]], axis=1),
                (((1,), (1,)), ((), ())),
                preferred_element_type=jnp.float32,
            )
        image[t] = result.astype(jnp.bfloat16)


def spread(pieces, target):
    at = 0
    for piece in pieces:
        size = piece.shape[0]
        target[at : at + size] = piece[...].astype(jnp.float32)
        at += size


def first_kernel(count, codes, floats, left, right, *refs):
    pieces, (image, state, codes_here, floats_here, semaphores, *mixed) = refs[:count], refs[count:]
    copies = fetch((codes, floats), (codes_here, floats_here), semaphores)
    spread(pieces, state)
    apply_operator(copies, codes_here, floats_here, state, left, right, mixed, image)


def rayleigh_update(before, images, after):
    shape = before[0].shape[1:]
    intersection = jnp.zeros(shape, jnp.float32)
    squares = jnp.zeros(shape, jnp.float32)
    at = 0
    flat = []
    for piece in before:
        flat += [(piece, s) for s in range(piece.shape[0])]
    pictures = []
    for piece in images:
        pictures += [(piece, s) for s in range(piece.shape[0])]
    for (piece, s), (picture, p) in zip(flat, pictures):
        value = piece[s].astype(jnp.float32)
        intersection += value * picture[p].astype(jnp.float32)
        squares += value * value
    energy = jnp.sum(intersection) / jnp.sum(squares)
    growth = 1.0 + STEP * energy
    for (piece, s), (picture, p) in zip(flat, pictures):
        after[at] = growth * piece[s].astype(jnp.float32) - STEP * picture[p].astype(jnp.float32)
        at += 1
    return energy


def middle_kernel(states, count, codes, floats, left, right, *refs):
    before, images = refs[:states], refs[states : states + count]
    energy, state, image, codes_here, floats_here, semaphores, *mixed = refs[states + count :]
    copies = fetch((codes, floats), (codes_here, floats_here), semaphores)
    energy[...] = jnp.full(energy.shape, rayleigh_update(before, images, state))
    apply_operator(copies, codes_here, floats_here, state, left, right, mixed, image)


def last_kernel(states, count, codes, floats, ranks, left, right, *refs):
    before, images = refs[:states], refs[states : states + count]
    energy, own, image, sums, state, codes_here, floats_here, ranks_here, semaphores, *mixed = refs[states + count :]
    copies = fetch((codes, floats, ranks), (codes_here, floats_here, ranks_here), semaphores)
    energy[...] = jnp.full(energy.shape, rayleigh_update(before, images, state))
    apply_operator(copies, codes_here, floats_here, state, left, right, mixed, image)
    blocks, size = image.shape[0], image.shape[1]
    intersection = jnp.zeros((size, size), jnp.float32)
    squares = jnp.zeros((size, size), jnp.float32)
    for t in range(blocks):
        value = state[t]
        intersection += value * image[t].astype(jnp.float32)
        squares += value * value
    intersection, squares = jnp.sum(intersection), jnp.sum(squares)
    here = jnp.where(squares > 1e-30, intersection / jnp.maximum(squares, 1e-30), 0.0)
    growth = 1.0 + STEP * here
    column = lax.broadcasted_iota(jnp.int32, (size, size), 1)
    dd = jnp.zeros((size, size), jnp.float32)
    dc = jnp.zeros((size, size), jnp.float32)
    cc = jnp.zeros((size, size), jnp.float32)
    for t in range(blocks):
        keep = column < ranks_here[0, t]
        value = jnp.where(keep, state[t], 0.0)
        picture = jnp.where(keep, image[t].astype(jnp.float32), 0.0)
        own[t] = value
        image[t] = picture.astype(jnp.bfloat16)
        moved = growth * value - STEP * picture
        dd += moved * moved
        dc += moved * value
        cc += value * value
    row = lax.broadcasted_iota(jnp.int32, sums.shape, 1)
    result = jnp.zeros(sums.shape, jnp.float32)
    for at, number in enumerate([intersection, squares, here, jnp.sum(dd), jnp.sum(dc), jnp.sum(cc)]):
        result = jnp.where(row == at, number, result)
    sums[...] = result


def finish_kernel(steps, count, entries, own, image, *refs):
    earlier, gathered, (energies, kept) = refs[:steps], refs[steps : steps + count], refs[steps + count :]
    rows = []
    for piece in gathered:
        rows += [piece[s] for s in range(piece.shape[0])]
    intersection = sum(row[0:1, :] for row in rows)
    squares = sum(row[1:2, :] for row in rows)
    total = intersection / squares
    kept_sq = jnp.zeros_like(total)
    for row in rows:
        shift = STEP * (total - row[2:3, :])
        kept_sq += row[3:4, :] + 2.0 * shift * row[4:5, :] + shift * shift * row[5:6, :]
    column = lax.broadcasted_iota(jnp.int32, total.shape, 1)
    listed = total
    for step, energy in enumerate(earlier):
        listed = jnp.where(column == step, energy[...], listed)
    energies[...] = listed[:, : steps + 1]
    growth = 1.0 + STEP * total
    scale = 1.0 / jnp.sqrt(jnp.maximum(kept_sq, 0.0) / entries + EPSILON)
    for t in range(image.shape[0]):
        kept[t] = ((growth * own[t] - STEP * image[t].astype(jnp.float32)) * scale).astype(jnp.bfloat16)


def local(initial_state, left_blocks, right_blocks, sources, channels, couplings, kept_rank):
    start = initial_state[0]
    left = left_blocks[0]
    right = lax.ppermute(right_blocks[0], "seg", [(0, 1), (1, 0)])
    blocks, size = start.shape[0], start.shape[1]
    width = left.shape[1]
    sectors = blocks * lax.axis_size("sec")
    entries = float(sectors * size * size)
    devices = lax.axis_size("sec")
    pairs = sources.shape[2]
    params = pltpu.CompilerParams(vmem_limit_bytes=32 * 2**20)
    ints = jax.ShapeDtypeStruct((blocks, pairs), jnp.int32)
    floats = jax.ShapeDtypeStruct((blocks, pairs), jnp.float32)
    codes, couplings, left = pl.pallas_call(
        functools.partial(prepare_kernel, devices),
        out_shape=(ints, floats, jax.ShapeDtypeStruct(left.shape, left.dtype)),
        in_specs=[HBM] * 4,
        out_specs=(SMEM, SMEM, VMEM),
        scratch_shapes=[
            pltpu.SMEM(ints.shape, jnp.int32),
            pltpu.SMEM(ints.shape, jnp.int32),
            pltpu.SMEM(ints.shape, jnp.float32),
            pltpu.SMEM((blocks, width + 1), jnp.int32),
            pltpu.SemaphoreType.DMA((4,)),
        ],
        compiler_params=params,
        name="prepare",
    )(sources[0], channels[0], couplings[0], left)

    own_type = jax.ShapeDtypeStruct((blocks, size, size), jnp.bfloat16)
    number = jax.ShapeDtypeStruct((1, 128), jnp.float32)
    whole = (sectors, size, size)
    tables = [pltpu.SMEM(ints.shape, jnp.int32), pltpu.SMEM(floats.shape, jnp.float32)]
    mixed = [pltpu.VMEM((width, size, size), jnp.bfloat16)] * blocks

    states = gather(start)
    image = pl.pallas_call(
        functools.partial(first_kernel, len(states)),
        out_shape=own_type,
        in_specs=[ANY, ANY] + [VMEM] * (2 + len(states)),
        out_specs=VMEM,
        scratch_shapes=[pltpu.VMEM(whole, jnp.float32), *tables, pltpu.SemaphoreType.DMA((2,)), *mixed],
        compiler_params=params,
        name="first_image",
    )(codes, couplings, left, right, *states)
    energies = []
    for _ in range(1, ITERS - 1):
        images = gather(image)
        energy, state, image = pl.pallas_call(
            functools.partial(middle_kernel, len(states), len(images)),
            out_shape=(number, jax.ShapeDtypeStruct(whole, jnp.float32), own_type),
            in_specs=[ANY, ANY] + [VMEM] * (2 + len(states) + len(images)),
            out_specs=(VMEM, VMEM, VMEM),
            scratch_shapes=[*tables, pltpu.SemaphoreType.DMA((2,)), *mixed],
            compiler_params=params,
            name="middle_image",
        )(codes, couplings, left, right, *states, *images)
        states = [state]
        energies.append(energy)
    images = gather(image)
    energy, own, image, sums = pl.pallas_call(
        functools.partial(last_kernel, len(states), len(images)),
        out_shape=(
            number,
            jax.ShapeDtypeStruct((blocks, size, size), jnp.float32),
            own_type,
            jax.ShapeDtypeStruct((1, 8, 128), jnp.float32),
        ),
        in_specs=[ANY, ANY, ANY] + [VMEM] * (2 + len(states) + len(images)),
        out_specs=(VMEM, VMEM, VMEM, VMEM),
        scratch_shapes=[
            pltpu.VMEM(whole, jnp.float32),
            *tables,
            pltpu.SMEM((1, blocks), jnp.int32),
            pltpu.SemaphoreType.DMA((3,)),
            *mixed,
        ],
        compiler_params=params,
        name="last_image",
    )(codes, couplings, kept_rank, left, right, *states, *images)
    energies.append(energy)
    gathered = gather_small(sums)
    energies, kept = pl.pallas_call(
        functools.partial(finish_kernel, len(energies), len(gathered), entries),
        out_shape=(jax.ShapeDtypeStruct((1, ITERS), jnp.float32), own_type),
        in_specs=[VMEM] * (2 + len(energies) + len(gathered)),
        out_specs=(VMEM, VMEM),
        compiler_params=params,
        name="finish",
    )(own, image, *energies, *gathered)
    return kept[None], energies


def solution(mesh):
    return jax.shard_map(
        local,
        mesh=mesh,
        in_specs=(
            P(("parts", "seg"), "sec", None, None),
            P(("parts", "seg"), "sec", None, None, None),
            P(("parts", "seg"), "sec", None, None, None),
            P(("parts", "seg"), "sec", None),
            P(("parts", "seg"), "sec", None),
            P(("parts", "seg"), "sec", None),
            P(("parts", "seg"), "sec"),
        ),
        out_specs=(P(("parts", "seg"), "sec", None, None), P(("parts", "seg"), None)),
        check_vma=False,
    )
```

```python
import functools

import jax
import jax.numpy as jnp
from jax import lax
from jax.experimental import pallas as pl
from jax.experimental.pallas import tpu as pltpu
from jax.sharding import PartitionSpec as P

ITERS = 3
STEP = 0.5
EPSILON = 1e-06
SMEM = pl.BlockSpec(memory_space=pltpu.SMEM)
VMEM = pl.BlockSpec(memory_space=pltpu.VMEM)
ANY = pl.BlockSpec(memory_space=pl.ANY)
HBM = pl.BlockSpec(memory_space=pltpu.HBM)
APART = (0, 4, 1, 2, 3, 5, 6, 7)


def hop(block, distance):
    count = lax.axis_size("sec")
    return lax.ppermute(block, "sec", [(a, a ^ distance) for a in range(count)])


def gather(block):
    if lax.axis_size("sec") != len(APART):
        return [lax.all_gather(block, "sec", axis=0, tiled=True)]
    relayed = hop(block, 4)
    near = [hop(block, distance) for distance in (1, 2, 3)]
    return [block, relayed] + near + [hop(relayed, distance) for distance in (1, 2, 3)]


def slot(sector, blocks, devices, here):
    if devices != len(APART):
        return sector
    apart = lax.div(sector, blocks) ^ here
    place = jnp.int32(0)
    for position in range(1, devices):
        place = jnp.where(apart == APART[position], position, place)
    return place * blocks + lax.rem(sector, blocks)


def prepare_kernel(devices, *refs):
    arguments, left, (codes, floats, near), scratch = refs[:3], refs[3], refs[4:7], refs[7:]
    sources, channels, couplings, starts, semaphores = scratch
    copies = fetch((*arguments, left), (sources, channels, couplings, near), semaphores)
    blocks, pairs = sources.shape
    width = near.shape[1]
    here = lax.axis_index("sec")
    seen = 1 << 16
    for w in range(width + 1):
        for t in range(blocks):
            starts[t, w] = 0
    for copy in copies[:3]:
        copy.wait()

    def count(k, carry):
        for t in range(blocks):
            starts[t, channels[t, k] + 1] += 1
        return carry

    def add(w, totals):
        totals = tuple(totals[t] + starts[t, w] for t in range(blocks))
        for t in range(blocks):
            starts[t, w] = totals[t]
        return totals

    def put(k, carry):
        for t in range(blocks):
            channel = channels[t, k]
            mark = starts[t, channel]
            to = mark & (seen - 1)
            starts[t, channel] = (to + 1) | seen
            same = lax.shift_right_logical(mark, 16)
            code = slot(sources[t, k], blocks, devices, here)
            codes[t, to] = (code << 16) | (channel << 1) | same
            floats[t, to] = couplings[t, k]
        return carry

    lax.fori_loop(0, pairs, count, 0, unroll=4)
    lax.fori_loop(0, width + 1, add, (jnp.int32(0),) * blocks, unroll=5)
    lax.fori_loop(0, pairs, put, 0, unroll=2)
    copies[3].wait()


def fetch(sources, targets, semaphores):
    copies = [
        pltpu.make_async_copy(source, target, semaphores.at[at])
        for at, (source, target) in enumerate(zip(sources, targets))
    ]
    for copy in copies:
        copy.start()
    return copies


def apply_operator(copies, codes, floats, state, left, right, mixed, image):
    blocks, width = left.shape[0], left.shape[1]
    pairs = floats.shape[1]
    for t in range(blocks):
        mixed[t][...] = jnp.zeros_like(mixed[t])
    for copy in copies:
        copy.wait()
    for t in range(blocks):
        total = jnp.zeros(state.shape[1:], jnp.float32)
        for k in range(pairs):
            code = codes[t, k]
            term = floats[t, k] * state[lax.shift_right_logical(code, 16)]
            total = term + jnp.where((code & 1) == 1, total, 0.0)
            mixed[t][lax.shift_right_logical(code, 1) & 0x7FFF] = total.astype(jnp.bfloat16)
    for t in range(blocks):
        result = jnp.zeros(image.shape[1:], jnp.float32)
        for w in range(0, width, 2):
            halves = [
                jnp.dot(left[t, v], mixed[t][v], preferred_element_type=jnp.float32).astype(jnp.bfloat16)
                for v in (w, w + 1)
            ]
            result += lax.dot_general(
                jnp.concatenate(halves, axis=1),
                jnp.concatenate([right[t, w], right[t, w + 1]], axis=1),
                (((1,), (1,)), ((), ())),
                preferred_element_type=jnp.float32,
            )
        image[t] = result.astype(jnp.bfloat16)


def spread(pieces, target):
    at = 0
    for piece in pieces:
        size = piece.shape[0]
        target[at : at + size] = piece[...].astype(jnp.float32)
        at += size


def first_kernel(count, codes, floats, left, right, *refs):
    pieces, (image, state, codes_here, floats_here, semaphores, *mixed) = refs[:count], refs[count:]
    copies = fetch((codes, floats), (codes_here, floats_here), semaphores)
    spread(pieces, state)
    apply_operator(copies, codes_here, floats_here, state, left, right, mixed, image)


def rayleigh_update(before, images, after):
    shape = before[0].shape[1:]
    intersection = jnp.zeros(shape, jnp.float32)
    squares = jnp.zeros(shape, jnp.float32)
    at = 0
    flat = []
    for piece in before:
        flat += [(piece, s) for s in range(piece.shape[0])]
    pictures = []
    for piece in images:
        pictures += [(piece, s) for s in range(piece.shape[0])]
    for (piece, s), (picture, p) in zip(flat, pictures):
        value = piece[s].astype(jnp.float32)
        intersection += value * picture[p].astype(jnp.float32)
        squares += value * value
    energy = jnp.sum(intersection) / jnp.sum(squares)
    growth = 1.0 + STEP * energy
    for (piece, s), (picture, p) in zip(flat, pictures):
        after[at] = growth * piece[s].astype(jnp.float32) - STEP * picture[p].astype(jnp.float32)
        at += 1
    return energy


def middle_kernel(states, count, codes, floats, left, right, *refs):
    before, images = refs[:states], refs[states : states + count]
    energy, state, image, codes_here, floats_here, semaphores, *mixed = refs[states + count :]
    copies = fetch((codes, floats), (codes_here, floats_here), semaphores)
    energy[...] = jnp.full(energy.shape, rayleigh_update(before, images, state))
    apply_operator(copies, codes_here, floats_here, state, left, right, mixed, image)


def last_kernel(states, count, codes, floats, ranks, left, right, *refs):
    before, images = refs[:states], refs[states : states + count]
    energy, own, image, sums, state, codes_here, floats_here, ranks_here, semaphores, *mixed = refs[states + count :]
    copies = fetch((codes, floats, ranks), (codes_here, floats_here, ranks_here), semaphores)
    energy[...] = jnp.full(energy.shape, rayleigh_update(before, images, state))
    apply_operator(copies, codes_here, floats_here, state, left, right, mixed, image)
    blocks, size = image.shape[0], image.shape[1]
    intersection = jnp.zeros((size, size), jnp.float32)
    squares = jnp.zeros((size, size), jnp.float32)
    for t in range(blocks):
        value = state[t]
        intersection += value * image[t].astype(jnp.float32)
        squares += value * value
    intersection, squares = jnp.sum(intersection), jnp.sum(squares)
    here = jnp.where(squares > 1e-30, intersection / jnp.maximum(squares, 1e-30), 0.0)
    growth = 1.0 + STEP * here
    column = lax.broadcasted_iota(jnp.int32, (size, size), 1)
    dd = jnp.zeros((size, size), jnp.float32)
    dc = jnp.zeros((size, size), jnp.float32)
    cc = jnp.zeros((size, size), jnp.float32)
    for t in range(blocks):
        keep = column < ranks_here[0, t]
        value = jnp.where(keep, state[t], 0.0)
        picture = jnp.where(keep, image[t].astype(jnp.float32), 0.0)
        own[t] = value
        image[t] = picture.astype(jnp.bfloat16)
        moved = growth * value - STEP * picture
        dd += moved * moved
        dc += moved * value
        cc += value * value
    row = lax.broadcasted_iota(jnp.int32, sums.shape, 1)
    result = jnp.zeros(sums.shape, jnp.float32)
    for at, number in enumerate([intersection, squares, here, jnp.sum(dd), jnp.sum(dc), jnp.sum(cc)]):
        result = jnp.where(row == at, number, result)
    sums[...] = result


def finish_kernel(steps, entries, own, image, gathered, *refs):
    earlier, (energies, kept) = refs[:steps], refs[steps:]
    rows = [gathered[device] for device in range(gathered.shape[0])]
    intersection = sum(row[0:1, :] for row in rows)
    squares = sum(row[1:2, :] for row in rows)
    total = intersection / squares
    kept_sq = jnp.zeros_like(total)
    for row in rows:
        shift = STEP * (total - row[2:3, :])
        kept_sq += row[3:4, :] + 2.0 * shift * row[4:5, :] + shift * shift * row[5:6, :]
    column = lax.broadcasted_iota(jnp.int32, total.shape, 1)
    listed = total
    for step, energy in enumerate(earlier):
        listed = jnp.where(column == step, energy[...], listed)
    energies[...] = listed[:, : steps + 1]
    growth = 1.0 + STEP * total
    scale = 1.0 / jnp.sqrt(jnp.maximum(kept_sq, 0.0) / entries + EPSILON)
    for t in range(image.shape[0]):
        kept[t] = ((growth * own[t] - STEP * image[t].astype(jnp.float32)) * scale).astype(jnp.bfloat16)


def local(initial_state, left_blocks, right_blocks, sources, channels, couplings, kept_rank):
    start = initial_state[0]
    left = left_blocks[0]
    right = lax.ppermute(right_blocks[0], "seg", [(0, 1), (1, 0)])
    blocks, size = start.shape[0], start.shape[1]
    width = left.shape[1]
    sectors = blocks * lax.axis_size("sec")
    entries = float(sectors * size * size)
    devices = lax.axis_size("sec")
    pairs = sources.shape[2]
    params = pltpu.CompilerParams(vmem_limit_bytes=32 * 2**20)
    ints = jax.ShapeDtypeStruct((blocks, pairs), jnp.int32)
    floats = jax.ShapeDtypeStruct((blocks, pairs), jnp.float32)
    codes, couplings, left = pl.pallas_call(
        functools.partial(prepare_kernel, devices),
        out_shape=(ints, floats, jax.ShapeDtypeStruct(left.shape, left.dtype)),
        in_specs=[HBM] * 4,
        out_specs=(SMEM, SMEM, VMEM),
        scratch_shapes=[
            pltpu.SMEM(ints.shape, jnp.int32),
            pltpu.SMEM(ints.shape, jnp.int32),
            pltpu.SMEM(ints.shape, jnp.float32),
            pltpu.SMEM((blocks, width + 1), jnp.int32),
            pltpu.SemaphoreType.DMA((4,)),
        ],
        compiler_params=params,
        name="prepare",
    )(*(pltpu.with_memory_space_constraint(block, pltpu.HBM) for block in (sources[0], channels[0], couplings[0], left)))

    own_type = jax.ShapeDtypeStruct((blocks, size, size), jnp.bfloat16)
    number = jax.ShapeDtypeStruct((1, 128), jnp.float32)
    whole = (sectors, size, size)
    tables = [pltpu.SMEM(ints.shape, jnp.int32), pltpu.SMEM(floats.shape, jnp.float32)]
    mixed = [pltpu.VMEM((width, size, size), jnp.bfloat16)] * blocks

    states = gather(start)
    image = pl.pallas_call(
        functools.partial(first_kernel, len(states)),
        out_shape=own_type,
        in_specs=[ANY, ANY] + [VMEM] * (2 + len(states)),
        out_specs=VMEM,
        scratch_shapes=[pltpu.VMEM(whole, jnp.float32), *tables, pltpu.SemaphoreType.DMA((2,)), *mixed],
        compiler_params=params,
        name="first_image",
    )(codes, couplings, left, right, *states)
    energies = []
    for _ in range(1, ITERS - 1):
        images = gather(image)
        energy, state, image = pl.pallas_call(
            functools.partial(middle_kernel, len(states), len(images)),
            out_shape=(number, jax.ShapeDtypeStruct(whole, jnp.float32), own_type),
            in_specs=[ANY, ANY] + [VMEM] * (2 + len(states) + len(images)),
            out_specs=(VMEM, VMEM, VMEM),
            scratch_shapes=[*tables, pltpu.SemaphoreType.DMA((2,)), *mixed],
            compiler_params=params,
            name="middle_image",
        )(codes, couplings, left, right, *states, *images)
        states = [state]
        energies.append(energy)
    images = gather(image)
    energy, own, image, sums = pl.pallas_call(
        functools.partial(last_kernel, len(states), len(images)),
        out_shape=(
            number,
            jax.ShapeDtypeStruct((blocks, size, size), jnp.float32),
            own_type,
            jax.ShapeDtypeStruct((devices, 8, 128), jnp.float32),
        ),
        in_specs=[ANY, ANY, ANY] + [VMEM] * (2 + len(states) + len(images)),
        out_specs=(VMEM, VMEM, VMEM, VMEM),
        scratch_shapes=[
            pltpu.VMEM(whole, jnp.float32),
            *tables,
            pltpu.SMEM((1, blocks), jnp.int32),
            pltpu.SemaphoreType.DMA((3,)),
            *mixed,
        ],
        compiler_params=params,
        name="last_image",
    )(codes, couplings, kept_rank, left, right, *states, *images)
    energies.append(energy)
    gathered = lax.all_to_all(sums, "sec", 0, 0)
    energies, kept = pl.pallas_call(
        functools.partial(finish_kernel, len(energies), entries),
        out_shape=(jax.ShapeDtypeStruct((1, ITERS), jnp.float32), own_type),
        in_specs=[VMEM] * (3 + len(energies)),
        out_specs=(VMEM, VMEM),
        compiler_params=params,
        name="finish",
    )(own, image, gathered, *energies)
    return kept[None], energies


def solution(mesh):
    return jax.shard_map(
        local,
        mesh=mesh,
        in_specs=(
            P(("parts", "seg"), "sec", None, None),
            P(("parts", "seg"), "sec", None, None, None),
            P(("parts", "seg"), "sec", None, None, None),
            P(("parts", "seg"), "sec", None),
            P(("parts", "seg"), "sec", None),
            P(("parts", "seg"), "sec", None),
            P(("parts", "seg"), "sec"),
        ),
        out_specs=(P(("parts", "seg"), "sec", None, None), P(("parts", "seg"), None)),
        check_vma=False,
    )
```

```python
import functools

import jax
import jax.numpy as jnp
from jax import lax
from jax.experimental import pallas as pl
from jax.experimental.pallas import tpu as pltpu
from jax.sharding import PartitionSpec as P

ITERS = 3
STEP = 0.5
EPSILON = 1e-06
SMEM = pl.BlockSpec(memory_space=pltpu.SMEM)
VMEM = pl.BlockSpec(memory_space=pltpu.VMEM)
ANY = pl.BlockSpec(memory_space=pl.ANY)
HBM = pl.BlockSpec(memory_space=pltpu.HBM)
APART = (0, 4, 1, 2, 3, 5, 6, 7)


def hop(block, distance):
    count = lax.axis_size("sec")
    return lax.ppermute(block, "sec", [(a, a ^ distance) for a in range(count)])


def gather(block):
    if lax.axis_size("sec") != len(APART):
        return [lax.all_gather(block, "sec", axis=0, tiled=True)]
    relayed = hop(block, 4)
    near = [hop(block, distance) for distance in (1, 2, 3)]
    return [block, relayed] + near + [hop(relayed, distance) for distance in (1, 2, 3)]


def cross(block, distance):
    count = lax.axis_size("sec")
    route = [(a, count + (a ^ distance)) for a in range(count)] + [(count + a, a ^ distance) for a in range(count)]
    return lax.ppermute(block, ("seg", "sec"), route)


def gather_small(block):
    if lax.axis_size("sec") != len(APART):
        return [lax.all_gather(block, "sec", axis=0, tiled=True)]
    line = jnp.concatenate([cross(block, distance) for distance in (0, 1, 2, 3)])
    return [cross(line, 0), cross(line, 4)]


def slot(sector, blocks, devices, here):
    if devices != len(APART):
        return sector
    owner = sum((sector >= blocks * device).astype(jnp.int32) for device in range(1, devices))
    apart = owner ^ here
    place = jnp.zeros_like(sector)
    for position in range(1, devices):
        place = jnp.where(apart == APART[position], position, place)
    return place * blocks + sector - owner * blocks


def code_bits(width):
    return (2 * width - 1).bit_length()


def prepare_kernel(devices, *refs):
    arguments, left, (codes, floats, near), (sources, channels, couplings, semaphores) = refs[:3], refs[3], refs[4:7], refs[7:]
    copies = fetch((*arguments, left), (sources, channels, couplings, near), semaphores)
    blocks, pairs = sources.shape
    width = near.shape[1]
    here = lax.axis_index("sec")
    down = lax.broadcasted_iota(jnp.int32, (pairs, pairs), 0)
    across = lax.broadcasted_iota(jnp.int32, (pairs, pairs), 1)

    def column(row):
        return jnp.sum(jnp.where(down == across, row, 0.0), axis=1, keepdims=True)

    for copy in copies[:3]:
        copy.wait()
    for t in range(blocks):
        channel = channels[t : t + 1, :].astype(jnp.float32)
        place = slot(sources[t : t + 1, :], blocks, devices, here).astype(jnp.float32)
        mine = column(channel)
        earlier = (channel == mine) & (across < down)
        rank = jnp.sum(jnp.where((channel < mine) | earlier, 1.0, 0.0), axis=1, keepdims=True)
        same = jnp.max(jnp.where(earlier, 1.0, 0.0), axis=1, keepdims=True)
        code = column(place) * float(1 << code_bits(width)) + 2.0 * mine + same
        chosen = rank == across.astype(jnp.float32)
        codes[t : t + 1, :] = jnp.sum(jnp.where(chosen, code, 0.0), axis=0, keepdims=True).astype(jnp.int32)
        floats[t : t + 1, :] = jnp.sum(jnp.where(chosen, column(couplings[t : t + 1, :]), 0.0), axis=0, keepdims=True)
    copies[3].wait()


def fetch(sources, targets, semaphores):
    copies = [
        pltpu.make_async_copy(source, target, semaphores.at[at])
        for at, (source, target) in enumerate(zip(sources, targets))
    ]
    for copy in copies:
        copy.start()
    return copies


def mixing(t, codes, floats, state, mixed):
    pairs = floats.shape[1]
    width, size = mixed[t].shape[0], mixed[t].shape[1]
    bits = code_bits(width)
    for first in range(0, size, size // 2):
        rows = slice(first, first + size // 2)
        total = jnp.zeros((size // 2, size), jnp.float32)
        for k in range(pairs):
            code = codes[t, k]
            term = floats[t, k] * state[lax.shift_right_logical(code, bits), rows]
            total = term + jnp.where((code & 1) == 1, total, 0.0)
            channel = lax.shift_right_logical(code, 1) & ((1 << (bits - 1)) - 1)
            mixed[t][channel, rows] = total.astype(jnp.bfloat16)
            yield


def apply_operator(copies, codes, floats, state, left, right, mixed, image):
    blocks, width = left.shape[0], left.shape[1]
    for t in range(blocks):
        mixed[t][...] = jnp.zeros_like(mixed[t])
    for copy in copies:
        copy.wait()
    steps = [mixing(t, codes, floats, state, mixed) for t in range(blocks)]
    for _ in steps[0]:
        pass
    share = -(-4 * floats.shape[1] // width)
    for t in range(blocks):
        result = jnp.zeros(image.shape[1:], jnp.float32)
        for w in range(0, width, 2):
            halves = [
                jnp.dot(left[t, v], mixed[t][v], preferred_element_type=jnp.float32).astype(jnp.bfloat16)
                for v in (w, w + 1)
            ]
            result += lax.dot_general(
                jnp.concatenate(halves, axis=1),
                jnp.concatenate([right[t, w], right[t, w + 1]], axis=1),
                (((1,), (1,)), ((), ())),
                preferred_element_type=jnp.float32,
            )
            if t + 1 < blocks:
                for _ in range(share):
                    next(steps[t + 1], None)
        image[t] = result.astype(jnp.bfloat16)
        if t + 1 < blocks:
            for _ in steps[t + 1]:
                pass


def spread(pieces, target):
    at = 0
    for piece in pieces:
        size = piece.shape[0]
        target[at : at + size] = piece[...].astype(jnp.float32)
        at += size


def first_kernel(count, codes, floats, left, right, *refs):
    pieces, (image, state, codes_here, floats_here, semaphores, *mixed) = refs[:count], refs[count:]
    copies = fetch((codes, floats), (codes_here, floats_here), semaphores)
    spread(pieces, state)
    apply_operator(copies, codes_here, floats_here, state, left, right, mixed, image)


def rayleigh_update(before, images, after):
    shape = before[0].shape[1:]
    intersection = jnp.zeros(shape, jnp.float32)
    squares = jnp.zeros(shape, jnp.float32)
    at = 0
    flat = []
    for piece in before:
        flat += [(piece, s) for s in range(piece.shape[0])]
    pictures = []
    for piece in images:
        pictures += [(piece, s) for s in range(piece.shape[0])]
    for (piece, s), (picture, p) in zip(flat, pictures):
        value = piece[s].astype(jnp.float32)
        intersection += value * picture[p].astype(jnp.float32)
        squares += value * value
    energy = jnp.sum(intersection, keepdims=True) / jnp.sum(squares, keepdims=True)
    growth = 1.0 + STEP * energy
    for (piece, s), (picture, p) in zip(flat, pictures):
        after[at] = growth * piece[s].astype(jnp.float32) - STEP * picture[p].astype(jnp.float32)
        at += 1
    return energy


def middle_kernel(states, count, codes, floats, left, right, *refs):
    before, images = refs[:states], refs[states : states + count]
    energy, state, image, codes_here, floats_here, semaphores, *mixed = refs[states + count :]
    copies = fetch((codes, floats), (codes_here, floats_here), semaphores)
    energy[...] = jnp.broadcast_to(rayleigh_update(before, images, state), energy.shape)
    apply_operator(copies, codes_here, floats_here, state, left, right, mixed, image)


def last_kernel(states, count, codes, floats, ranks, left, right, *refs):
    before, images = refs[:states], refs[states : states + count]
    energy, own, image, sums, state, codes_here, floats_here, ranks_here, semaphores, *mixed = refs[states + count :]
    copies = fetch((codes, floats, ranks), (codes_here, floats_here, ranks_here), semaphores)
    energy[...] = jnp.broadcast_to(rayleigh_update(before, images, state), energy.shape)
    apply_operator(copies, codes_here, floats_here, state, left, right, mixed, image)
    blocks, size = image.shape[0], image.shape[1]
    intersection = jnp.zeros((size, size), jnp.float32)
    squares = jnp.zeros((size, size), jnp.float32)
    for t in range(blocks):
        value = state[t]
        intersection += value * image[t].astype(jnp.float32)
        squares += value * value
    intersection, squares = jnp.sum(intersection, keepdims=True), jnp.sum(squares, keepdims=True)
    here = jnp.where(squares > 1e-30, intersection / jnp.maximum(squares, 1e-30), 0.0)
    growth = 1.0 + STEP * here
    column = lax.broadcasted_iota(jnp.int32, (size, size), 1)
    dd = jnp.zeros((size, size), jnp.float32)
    dc = jnp.zeros((size, size), jnp.float32)
    cc = jnp.zeros((size, size), jnp.float32)
    for t in range(blocks):
        keep = column < ranks_here[0, t]
        value = jnp.where(keep, state[t], 0.0)
        picture = jnp.where(keep, image[t].astype(jnp.float32), 0.0)
        own[t] = value
        image[t] = picture.astype(jnp.bfloat16)
        moved = growth * value - STEP * picture
        dd += moved * moved
        dc += moved * value
        cc += value * value
    row = lax.broadcasted_iota(jnp.int32, sums.shape[1:], 0)
    result = jnp.zeros(sums.shape[1:], jnp.float32)
    kept = [jnp.sum(value, keepdims=True) for value in (dd, dc, cc)]
    for at, number in enumerate([intersection, squares, here, *kept]):
        result = jnp.where(row == at, number, result)
    sums[...] = jnp.broadcast_to(result, sums.shape)


def finish_kernel(steps, count, entries, own, image, *refs):
    earlier, gathered, (energies, kept) = refs[:steps], refs[steps : steps + count], refs[steps + count :]
    rows = [piece[device] for piece in gathered for device in range(piece.shape[0])]
    intersection = sum(row[0:1, :] for row in rows)
    squares = sum(row[1:2, :] for row in rows)
    total = intersection / squares
    kept_sq = jnp.zeros_like(total)
    for row in rows:
        shift = STEP * (total - row[2:3, :])
        kept_sq += row[3:4, :] + 2.0 * shift * row[4:5, :] + shift * shift * row[5:6, :]
    column = lax.broadcasted_iota(jnp.int32, total.shape, 1)
    listed = total
    for step, energy in enumerate(earlier):
        listed = jnp.where(column == step, energy[...], listed)
    energies[...] = listed[:, : steps + 1]
    growth = 1.0 + STEP * total
    scale = 1.0 / jnp.sqrt(jnp.maximum(kept_sq, 0.0) / entries + EPSILON)
    for t in range(image.shape[0]):
        kept[t] = ((growth * own[t] - STEP * image[t].astype(jnp.float32)) * scale).astype(jnp.bfloat16)


def local(initial_state, left_blocks, right_blocks, sources, channels, couplings, kept_rank):
    start = initial_state[0]
    left = left_blocks[0]
    right = lax.ppermute(right_blocks[0], "seg", [(0, 1), (1, 0)])
    blocks, size = start.shape[0], start.shape[1]
    width = left.shape[1]
    sectors = blocks * lax.axis_size("sec")
    entries = float(sectors * size * size)
    devices = lax.axis_size("sec")
    pairs = sources.shape[2]
    params = pltpu.CompilerParams(vmem_limit_bytes=32 * 2**20)
    ints = jax.ShapeDtypeStruct((blocks, pairs), jnp.int32)
    floats = jax.ShapeDtypeStruct((blocks, pairs), jnp.float32)
    codes, couplings, left = pl.pallas_call(
        functools.partial(prepare_kernel, devices),
        out_shape=(ints, floats, jax.ShapeDtypeStruct(left.shape, left.dtype)),
        in_specs=[HBM] * 4,
        out_specs=(VMEM, VMEM, VMEM),
        scratch_shapes=[
            pltpu.VMEM(ints.shape, jnp.int32),
            pltpu.VMEM(ints.shape, jnp.int32),
            pltpu.VMEM(ints.shape, jnp.float32),
            pltpu.SemaphoreType.DMA((4,)),
        ],
        compiler_params=params,
        name="prepare",
    )(*(pltpu.with_memory_space_constraint(block, pltpu.HBM) for block in (sources[0], channels[0], couplings[0], left)))

    own_type = jax.ShapeDtypeStruct((blocks, size, size), jnp.bfloat16)
    number = jax.ShapeDtypeStruct((1, 128), jnp.float32)
    whole = (sectors, size, size)
    tables = [pltpu.SMEM(ints.shape, jnp.int32), pltpu.SMEM(floats.shape, jnp.float32)]
    mixed = [pltpu.VMEM((width, size, size), jnp.bfloat16)] * blocks

    states = gather(start)
    image = pl.pallas_call(
        functools.partial(first_kernel, len(states)),
        out_shape=own_type,
        in_specs=[ANY, ANY] + [VMEM] * (2 + len(states)),
        out_specs=VMEM,
        scratch_shapes=[pltpu.VMEM(whole, jnp.float32), *tables, pltpu.SemaphoreType.DMA((2,)), *mixed],
        compiler_params=params,
        name="first_image",
    )(codes, couplings, left, right, *states)
    energies = []
    for _ in range(1, ITERS - 1):
        images = gather(image)
        energy, state, image = pl.pallas_call(
            functools.partial(middle_kernel, len(states), len(images)),
            out_shape=(number, jax.ShapeDtypeStruct(whole, jnp.float32), own_type),
            in_specs=[ANY, ANY] + [VMEM] * (2 + len(states) + len(images)),
            out_specs=(VMEM, VMEM, VMEM),
            scratch_shapes=[*tables, pltpu.SemaphoreType.DMA((2,)), *mixed],
            compiler_params=params,
            name="middle_image",
        )(codes, couplings, left, right, *states, *images)
        states = [state]
        energies.append(energy)
    images = gather(image)
    energy, own, image, sums = pl.pallas_call(
        functools.partial(last_kernel, len(states), len(images)),
        out_shape=(
            number,
            jax.ShapeDtypeStruct((blocks, size, size), jnp.float32),
            own_type,
            jax.ShapeDtypeStruct((1, 8, 128), jnp.float32),
        ),
        in_specs=[ANY, ANY, ANY] + [VMEM] * (2 + len(states) + len(images)),
        out_specs=(VMEM, VMEM, VMEM, VMEM),
        scratch_shapes=[
            pltpu.VMEM(whole, jnp.float32),
            *tables,
            pltpu.SMEM((1, blocks), jnp.int32),
            pltpu.SemaphoreType.DMA((3,)),
            *mixed,
        ],
        compiler_params=params,
        name="last_image",
    )(codes, couplings, kept_rank, left, right, *states, *images)
    energies.append(energy)
    gathered = gather_small(sums)
    energies, kept = pl.pallas_call(
        functools.partial(finish_kernel, len(energies), len(gathered), entries),
        out_shape=(jax.ShapeDtypeStruct((1, ITERS), jnp.float32), own_type),
        in_specs=[VMEM] * (2 + len(energies) + len(gathered)),
        out_specs=(VMEM, VMEM),
        compiler_params=params,
        name="finish",
    )(own, image, *energies, *gathered)
    return kept[None], energies


def solution(mesh):
    return jax.shard_map(
        local,
        mesh=mesh,
        in_specs=(
            P(("parts", "seg"), "sec", None, None),
            P(("parts", "seg"), "sec", None, None, None),
            P(("parts", "seg"), "sec", None, None, None),
            P(("parts", "seg"), "sec", None),
            P(("parts", "seg"), "sec", None),
            P(("parts", "seg"), "sec", None),
            P(("parts", "seg"), "sec"),
        ),
        out_specs=(P(("parts", "seg"), "sec", None, None), P(("parts", "seg"), None)),
        check_vma=False,
    )
```

```python
import functools

import jax
import jax.numpy as jnp
from jax import lax
from jax.experimental import pallas as pl
from jax.experimental.pallas import tpu as pltpu
from jax.sharding import PartitionSpec as P

ITERS = 3
STEP = 0.5
EPSILON = 1e-06
SMEM = pl.BlockSpec(memory_space=pltpu.SMEM)
VMEM = pl.BlockSpec(memory_space=pltpu.VMEM)
HBM = pl.BlockSpec(memory_space=pltpu.HBM)
APART = (0, 4, 3, 2, 1, 5, 6, 7)


def hop(block, distance):
    count = lax.axis_size("sec")
    return lax.ppermute(block, "sec", [(a, a ^ distance) for a in range(count)])


def gather(block):
    if lax.axis_size("sec") != len(APART):
        return [lax.all_gather(block, "sec", axis=0, tiled=True)]
    relayed = hop(block, 4)
    near = [hop(block, distance) for distance in (3, 2, 1)]
    return [block, relayed] + near + [hop(relayed, distance) for distance in (1, 2, 3)]


def cross(block, distance):
    count = lax.axis_size("sec")
    route = [(a, count + (a ^ distance)) for a in range(count)] + [(count + a, a ^ distance) for a in range(count)]
    return lax.ppermute(block, ("seg", "sec"), route)


def gather_small(block):
    if lax.axis_size("sec") != len(APART):
        return [lax.all_gather(block, "sec", axis=0, tiled=True)]
    line = jnp.concatenate([cross(block, distance) for distance in (0, 1, 2, 3)])
    return [cross(line, 0), cross(line, 4)]


def slot(sector, blocks, devices, here):
    if devices != len(APART):
        return sector
    owner = sum((sector >= blocks * device).astype(jnp.int32) for device in range(1, devices))
    apart = owner ^ here
    place = jnp.zeros_like(sector)
    for position in range(1, devices):
        place = jnp.where(apart == APART[position], position, place)
    return place * blocks + sector - owner * blocks


def code_bits(width):
    return (2 * width - 1).bit_length()


def prepare_kernel(devices, *refs):
    arguments, left, (codes, factors, near), (sources, channels, couplings, semaphores) = refs[:3], refs[3], refs[4:7], refs[7:]
    copies = fetch((*arguments, left), (sources, channels, couplings, near), semaphores)
    blocks, pairs = sources.shape
    width = near.shape[1]
    here = lax.axis_index("sec")
    down = lax.broadcasted_iota(jnp.int32, (pairs, pairs), 0)
    across = lax.broadcasted_iota(jnp.int32, (pairs, pairs), 1)

    def column(row):
        return jnp.sum(jnp.where(down == across, row, 0.0), axis=1, keepdims=True)

    for copy in copies[:3]:
        copy.wait()
    for t in range(blocks):
        channel = channels[t : t + 1, :].astype(jnp.float32)
        place = slot(sources[t : t + 1, :], blocks, devices, here).astype(jnp.float32)
        mine = column(channel)
        earlier = (channel == mine) & (across < down)
        rank = jnp.sum(jnp.where((channel < mine) | earlier, 1.0, 0.0), axis=1, keepdims=True)
        same = jnp.max(jnp.where(earlier, 1.0, 0.0), axis=1, keepdims=True)
        code = column(place) * float(1 << code_bits(width)) + 2.0 * mine + same
        chosen = rank == across.astype(jnp.float32)
        codes[t : t + 1, :] = jnp.sum(jnp.where(chosen, code, 0.0), axis=0, keepdims=True).astype(jnp.int32)
        factors[t : t + 1, :] = jnp.sum(jnp.where(chosen, column(couplings[t : t + 1, :]), 0.0), axis=0, keepdims=True)
    copies[3].wait()


def fetch(sources, targets, semaphores):
    copies = [
        pltpu.make_async_copy(source, target, semaphores.at[at])
        for at, (source, target) in enumerate(zip(sources, targets))
    ]
    for copy in copies:
        copy.start()
    return copies


def mixing(t, codes, factors, state, mixed):
    pairs = factors.shape[1]
    width, size = mixed[t].shape[0], mixed[t].shape[1]
    bits = code_bits(width)
    total = jnp.zeros((size, size), jnp.float32)
    for k in range(pairs):
        code = codes[t, k]
        term = factors[t, k] * state[lax.shift_right_logical(code, bits)]
        total = term + jnp.where((code & 1) == 1, total, 0.0)
        mixed[t][lax.shift_right_logical(code, 1) & ((1 << (bits - 1)) - 1)] = total.astype(jnp.bfloat16)


def apply_operator(codes, factors, state, left, right, mixed, image):
    blocks, width = left.shape[0], left.shape[1]
    for t in range(blocks):
        mixed[t][...] = jnp.zeros_like(mixed[t])
    for t in range(blocks):
        mixing(t, codes, factors, state, mixed)
    for t in range(blocks):
        result = jnp.zeros(image.shape[1:], jnp.float32)
        for w in range(0, width, 2):
            halves = [
                jnp.dot(left[t, v], mixed[t][v], preferred_element_type=jnp.float32).astype(jnp.bfloat16)
                for v in (w, w + 1)
            ]
            result += lax.dot_general(
                jnp.concatenate(halves, axis=1),
                jnp.concatenate([right[t, w], right[t, w + 1]], axis=1),
                (((1,), (1,)), ((), ())),
                preferred_element_type=jnp.float32,
            )
        image[t] = result.astype(jnp.bfloat16)


def spread(pieces, target):
    at = 0
    for piece in pieces:
        size = piece.shape[0]
        target[at : at + size] = piece[...].astype(jnp.float32)
        at += size


def first_kernel(count, codes, factors, left, right, *refs):
    pieces, (image, state, *mixed) = refs[:count], refs[count:]
    spread(pieces, state)
    apply_operator(codes[...], factors[...], state, left, right, mixed, image)


def rayleigh_update(before, images, after):
    shape = before[0].shape[1:]
    intersection = jnp.zeros(shape, jnp.float32)
    squares = jnp.zeros(shape, jnp.float32)
    at = 0
    flat = []
    for piece in before:
        flat += [(piece, s) for s in range(piece.shape[0])]
    pictures = []
    for piece in images:
        pictures += [(piece, s) for s in range(piece.shape[0])]
    for (piece, s), (picture, p) in zip(flat, pictures):
        value = piece[s].astype(jnp.float32)
        intersection += value * picture[p].astype(jnp.float32)
        squares += value * value
    energy = jnp.sum(intersection, keepdims=True) / jnp.sum(squares, keepdims=True)
    growth = 1.0 + STEP * energy
    for (piece, s), (picture, p) in zip(flat, pictures):
        after[at] = growth * piece[s].astype(jnp.float32) - STEP * picture[p].astype(jnp.float32)
        at += 1
    return energy


def middle_kernel(states, count, codes, factors, left, right, *refs):
    before, images = refs[:states], refs[states : states + count]
    energy, state, image, *mixed = refs[states + count :]
    energy[...] = jnp.broadcast_to(rayleigh_update(before, images, state), energy.shape)
    apply_operator(codes[...], factors[...], state, left, right, mixed, image)


def last_kernel(states, count, codes, factors, ranks, left, right, *refs):
    before, images = refs[:states], refs[states : states + count]
    energy, own, image, sums, state, *mixed = refs[states + count :]
    energy[...] = jnp.broadcast_to(rayleigh_update(before, images, state), energy.shape)
    apply_operator(codes[...], factors[...], state, left, right, mixed, image)
    blocks, size = image.shape[0], image.shape[1]
    intersection = jnp.zeros((size, size), jnp.float32)
    squares = jnp.zeros((size, size), jnp.float32)
    for t in range(blocks):
        value = state[t]
        intersection += value * image[t].astype(jnp.float32)
        squares += value * value
    intersection, squares = jnp.sum(intersection, keepdims=True), jnp.sum(squares, keepdims=True)
    here = jnp.where(squares > 1e-30, intersection / jnp.maximum(squares, 1e-30), 0.0)
    growth = 1.0 + STEP * here
    column = lax.broadcasted_iota(jnp.int32, (size, size), 1)
    dd = jnp.zeros((size, size), jnp.float32)
    dc = jnp.zeros((size, size), jnp.float32)
    cc = jnp.zeros((size, size), jnp.float32)
    for t in range(blocks):
        keep = column < ranks[0:1, t : t + 1]
        value = jnp.where(keep, state[t], 0.0)
        picture = jnp.where(keep, image[t].astype(jnp.float32), 0.0)
        own[t] = value
        image[t] = picture.astype(jnp.bfloat16)
        moved = growth * value - STEP * picture
        dd += moved * moved
        dc += moved * value
        cc += value * value
    row = lax.broadcasted_iota(jnp.int32, sums.shape[1:], 0)
    result = jnp.zeros(sums.shape[1:], jnp.float32)
    kept = [jnp.sum(value, keepdims=True) for value in (dd, dc, cc)]
    for at, number in enumerate([intersection, squares, here, *kept]):
        result = jnp.where(row == at, number, result)
    sums[...] = jnp.broadcast_to(result, sums.shape)


def finish_kernel(steps, count, entries, own, image, *refs):
    earlier, gathered, (energies, kept) = refs[:steps], refs[steps : steps + count], refs[steps + count :]
    rows = [piece[device] for piece in gathered for device in range(piece.shape[0])]
    intersection = sum(row[0:1, :] for row in rows)
    squares = sum(row[1:2, :] for row in rows)
    total = intersection / squares
    kept_sq = jnp.zeros_like(total)
    for row in rows:
        shift = STEP * (total - row[2:3, :])
        kept_sq += row[3:4, :] + 2.0 * shift * row[4:5, :] + shift * shift * row[5:6, :]
    column = lax.broadcasted_iota(jnp.int32, total.shape, 1)
    listed = total
    for step, energy in enumerate(earlier):
        listed = jnp.where(column == step, energy[...], listed)
    energies[...] = listed[:, : steps + 1]
    growth = 1.0 + STEP * total
    scale = 1.0 / jnp.sqrt(jnp.maximum(kept_sq, 0.0) / entries + EPSILON)
    for t in range(image.shape[0]):
        kept[t] = ((growth * own[t] - STEP * image[t].astype(jnp.float32)) * scale).astype(jnp.bfloat16)


def local(initial_state, left_blocks, right_blocks, sources, channels, couplings, kept_rank):
    start = initial_state[0]
    left = left_blocks[0]
    right = lax.ppermute(right_blocks[0], "seg", [(0, 1), (1, 0)])
    blocks, size = start.shape[0], start.shape[1]
    width = left.shape[1]
    sectors = blocks * lax.axis_size("sec")
    entries = float(sectors * size * size)
    devices = lax.axis_size("sec")
    pairs = sources.shape[2]
    params = pltpu.CompilerParams(vmem_limit_bytes=32 * 2**20)
    ints = jax.ShapeDtypeStruct((blocks, pairs), jnp.int32)
    factors = jax.ShapeDtypeStruct((blocks, pairs), jnp.float32)
    codes, factors, left = pl.pallas_call(
        functools.partial(prepare_kernel, devices),
        out_shape=(ints, factors, jax.ShapeDtypeStruct(left.shape, left.dtype)),
        in_specs=[HBM] * 4,
        out_specs=(VMEM, VMEM, VMEM),
        scratch_shapes=[
            pltpu.VMEM(ints.shape, jnp.int32),
            pltpu.VMEM(ints.shape, jnp.int32),
            pltpu.VMEM(ints.shape, jnp.float32),
            pltpu.SemaphoreType.DMA((4,)),
        ],
        compiler_params=params,
        name="prepare",
    )(*(pltpu.with_memory_space_constraint(block, pltpu.HBM) for block in (sources[0], channels[0], couplings[0], left)))

    own_type = jax.ShapeDtypeStruct((blocks, size, size), jnp.bfloat16)
    number = jax.ShapeDtypeStruct((1, 128), jnp.float32)
    whole = (sectors, size, size)
    mixed = [pltpu.VMEM((width, size, size), jnp.bfloat16)] * blocks

    states = gather(start)
    image = pl.pallas_call(
        functools.partial(first_kernel, len(states)),
        out_shape=own_type,
        in_specs=[VMEM] * (4 + len(states)),
        out_specs=VMEM,
        scratch_shapes=[pltpu.VMEM(whole, jnp.float32), *mixed],
        compiler_params=params,
        name="first_image",
    )(codes, factors, left, right, *states)
    energies = []
    for _ in range(1, ITERS - 1):
        images = gather(image)
        energy, state, image = pl.pallas_call(
            functools.partial(middle_kernel, len(states), len(images)),
            out_shape=(number, jax.ShapeDtypeStruct(whole, jnp.float32), own_type),
            in_specs=[VMEM] * (4 + len(states) + len(images)),
            out_specs=(VMEM, VMEM, VMEM),
            scratch_shapes=mixed,
            compiler_params=params,
            name="middle_image",
        )(codes, factors, left, right, *states, *images)
        states = [state]
        energies.append(energy)
    images = gather(image)
    energy, own, image, sums = pl.pallas_call(
        functools.partial(last_kernel, len(states), len(images)),
        out_shape=(
            number,
            jax.ShapeDtypeStruct((blocks, size, size), jnp.float32),
            own_type,
            jax.ShapeDtypeStruct((1, 8, 128), jnp.float32),
        ),
        in_specs=[VMEM] * (5 + len(states) + len(images)),
        out_specs=(VMEM, VMEM, VMEM, VMEM),
        scratch_shapes=[
            pltpu.VMEM(whole, jnp.float32),
            *mixed,
        ],
        compiler_params=params,
        name="last_image",
    )(codes, factors, kept_rank, left, right, *states, *images)
    energies.append(energy)
    gathered = gather_small(sums)
    energies, kept = pl.pallas_call(
        functools.partial(finish_kernel, len(energies), len(gathered), entries),
        out_shape=(jax.ShapeDtypeStruct((1, ITERS), jnp.float32), own_type),
        in_specs=[VMEM] * (2 + len(energies) + len(gathered)),
        out_specs=(VMEM, VMEM),
        compiler_params=params,
        name="finish",
    )(own, image, *energies, *gathered)
    return kept[None], energies


def solution(mesh):
    return jax.shard_map(
        local,
        mesh=mesh,
        in_specs=(
            P(("parts", "seg"), "sec", None, None),
            P(("parts", "seg"), "sec", None, None, None),
            P(("parts", "seg"), "sec", None, None, None),
            P(("parts", "seg"), "sec", None),
            P(("parts", "seg"), "sec", None),
            P(("parts", "seg"), "sec", None),
            P(("parts", "seg"), "sec"),
        ),
        out_specs=(P(("parts", "seg"), "sec", None, None), P(("parts", "seg"), None)),
        check_vma=False,
    )
```

```python
import functools

import jax
import jax.numpy as jnp
from jax import lax
from jax.experimental import pallas as pl
from jax.experimental.pallas import tpu as pltpu
from jax.sharding import PartitionSpec as P

ITERS = 3
STEP = 0.5
EPSILON = 1e-06
SMEM = pl.BlockSpec(memory_space=pltpu.SMEM)
VMEM = pl.BlockSpec(memory_space=pltpu.VMEM)
HBM = pl.BlockSpec(memory_space=pltpu.HBM)
APART = (0, 4, 3, 2, 1, 5, 6, 7)


def hop(block, distance):
    count = lax.axis_size("sec")
    return lax.ppermute(block, "sec", [(a, a ^ distance) for a in range(count)])


def gather(block):
    if lax.axis_size("sec") != len(APART):
        return [lax.all_gather(block, "sec", axis=0, tiled=True)]
    relayed = hop(block, 4)
    near = [hop(block, distance) for distance in (3, 2, 1)]
    return [block, relayed] + near + [hop(relayed, distance) for distance in (1, 2, 3)]


def cross(block, distance):
    count = lax.axis_size("sec")
    route = [(a, count + (a ^ distance)) for a in range(count)] + [(count + a, a ^ distance) for a in range(count)]
    return lax.ppermute(block, ("seg", "sec"), route)


def gather_small(block):
    if lax.axis_size("sec") != len(APART):
        return [lax.all_gather(block, "sec", axis=0, tiled=True)]
    line = jnp.concatenate([cross(block, distance) for distance in (0, 1, 2, 3)])
    return [cross(line, 0), cross(line, 4)]


def slot(sector, blocks, devices, here):
    if devices != len(APART):
        return sector
    owner = sum((sector >= blocks * device).astype(jnp.int32) for device in range(1, devices))
    apart = owner ^ here
    place = jnp.zeros_like(sector)
    for position in range(1, devices):
        place = jnp.where(apart == APART[position], position, place)
    return place * blocks + sector - owner * blocks


def first_slot(blocks):
    return 0 if lax.axis_size("sec") == len(APART) else lax.axis_index("sec") * blocks


def code_bits(width):
    return (2 * width - 1).bit_length()


def prepare_kernel(devices, *refs):
    arguments, left, (codes, factors, near), (sources, channels, couplings, semaphores) = refs[:3], refs[3], refs[4:7], refs[7:]
    copies = fetch((*arguments, left), (sources, channels, couplings, near), semaphores)
    blocks, pairs = sources.shape
    width = near.shape[1]
    here = lax.axis_index("sec")
    down = lax.broadcasted_iota(jnp.int32, (pairs, pairs), 0)
    across = lax.broadcasted_iota(jnp.int32, (pairs, pairs), 1)

    def column(row):
        return jnp.sum(jnp.where(down == across, row, 0.0), axis=1, keepdims=True)

    for copy in copies[:3]:
        copy.wait()
    for t in range(blocks):
        channel = channels[t : t + 1, :].astype(jnp.float32)
        place = slot(sources[t : t + 1, :], blocks, devices, here).astype(jnp.float32)
        mine = column(channel)
        earlier = (channel == mine) & (across < down)
        rank = jnp.sum(jnp.where((channel < mine) | earlier, 1.0, 0.0), axis=1, keepdims=True)
        same = jnp.max(jnp.where(earlier, 1.0, 0.0), axis=1, keepdims=True)
        code = column(place) * float(1 << code_bits(width)) + 2.0 * mine + same
        chosen = rank == across.astype(jnp.float32)
        codes[t : t + 1, :] = jnp.sum(jnp.where(chosen, code, 0.0), axis=0, keepdims=True).astype(jnp.int32)
        factors[t : t + 1, :] = jnp.sum(jnp.where(chosen, column(couplings[t : t + 1, :]), 0.0), axis=0, keepdims=True)
    copies[3].wait()


def fetch(sources, targets, semaphores):
    copies = [
        pltpu.make_async_copy(source, target, semaphores.at[at])
        for at, (source, target) in enumerate(zip(sources, targets))
    ]
    for copy in copies:
        copy.start()
    return copies


def mixing(t, codes, factors, state, mixed):
    pairs = factors.shape[1]
    width, size = mixed[t].shape[0], mixed[t].shape[1]
    bits = code_bits(width)
    total = jnp.zeros((size, size), jnp.float32)
    for k in range(pairs):
        code = codes[t, k]
        term = factors[t, k] * state[lax.shift_right_logical(code, bits)]
        total = term + jnp.where((code & 1) == 1, total, 0.0)
        mixed[t][lax.shift_right_logical(code, 1) & ((1 << (bits - 1)) - 1)] = total.astype(jnp.bfloat16)


def apply_operator(codes, factors, state, left, right, mixed, image):
    blocks, width = left.shape[0], left.shape[1]
    for t in range(blocks):
        mixed[t][...] = jnp.zeros_like(mixed[t])
    for t in range(blocks):
        mixing(t, codes, factors, state, mixed)
    for t in range(blocks):
        result = jnp.zeros(image.shape[1:], jnp.float32)
        for w in range(0, width, 2):
            halves = [
                jnp.dot(left[t, v], mixed[t][v], preferred_element_type=jnp.float32).astype(jnp.bfloat16)
                for v in (w, w + 1)
            ]
            result += lax.dot_general(
                jnp.concatenate(halves, axis=1),
                jnp.concatenate([right[t, w], right[t, w + 1]], axis=1),
                (((1,), (1,)), ((), ())),
                preferred_element_type=jnp.float32,
            )
        image[t] = result.astype(jnp.bfloat16)


def spread(pieces, target):
    at = 0
    for piece in pieces:
        size = piece.shape[0]
        target[at : at + size] = piece[...].astype(jnp.float32)
        at += size


def first_kernel(count, codes, factors, left, right, *refs):
    pieces, (image, state, *mixed) = refs[:count], refs[count:]
    spread(pieces, state)
    apply_operator(codes[...], factors[...], state, left, right, mixed, image)


def rayleigh_update(before, images, after):
    shape = before[0].shape[1:]
    intersection = jnp.zeros(shape, jnp.float32)
    squares = jnp.zeros(shape, jnp.float32)
    at = 0
    flat = []
    for piece in before:
        flat += [(piece, s) for s in range(piece.shape[0])]
    pictures = []
    for piece in images:
        pictures += [(piece, s) for s in range(piece.shape[0])]
    for (piece, s), (picture, p) in zip(flat, pictures):
        value = piece[s].astype(jnp.float32)
        intersection += value * picture[p].astype(jnp.float32)
        squares += value * value
    energy = jnp.sum(intersection, keepdims=True) / jnp.sum(squares, keepdims=True)
    growth = 1.0 + STEP * energy
    for (piece, s), (picture, p) in zip(flat, pictures):
        after[at] = growth * piece[s].astype(jnp.float32) - STEP * picture[p].astype(jnp.float32)
        at += 1
    return energy


def middle_kernel(states, count, codes, factors, left, right, *refs):
    before, images = refs[:states], refs[states : states + count]
    energy, state, image, *mixed = refs[states + count :]
    energy[...] = jnp.broadcast_to(rayleigh_update(before, images, state), energy.shape)
    apply_operator(codes[...], factors[...], state, left, right, mixed, image)


def last_kernel(states, count, codes, factors, ranks, left, right, *refs):
    before, images = refs[:states], refs[states : states + count]
    energy, own, image, sums, state, *mixed = refs[states + count :]
    energy[...] = jnp.broadcast_to(rayleigh_update(before, images, state), energy.shape)
    apply_operator(codes[...], factors[...], state, left, right, mixed, image)
    blocks, size = image.shape[0], image.shape[1]
    first = first_slot(blocks)
    intersection = jnp.zeros((size, size), jnp.float32)
    squares = jnp.zeros((size, size), jnp.float32)
    for t in range(blocks):
        value = state[first + t]
        intersection += value * image[t].astype(jnp.float32)
        squares += value * value
    intersection, squares = jnp.sum(intersection, keepdims=True), jnp.sum(squares, keepdims=True)
    here = jnp.where(squares > 1e-30, intersection / jnp.maximum(squares, 1e-30), 0.0)
    growth = 1.0 + STEP * here
    column = lax.broadcasted_iota(jnp.int32, (size, size), 1)
    dd = jnp.zeros((size, size), jnp.float32)
    dc = jnp.zeros((size, size), jnp.float32)
    cc = jnp.zeros((size, size), jnp.float32)
    for t in range(blocks):
        keep = column < ranks[0:1, t : t + 1]
        value = jnp.where(keep, state[first + t], 0.0)
        picture = jnp.where(keep, image[t].astype(jnp.float32), 0.0)
        own[t] = value
        image[t] = picture.astype(jnp.bfloat16)
        moved = growth * value - STEP * picture
        dd += moved * moved
        dc += moved * value
        cc += value * value
    row = lax.broadcasted_iota(jnp.int32, sums.shape[1:], 0)
    result = jnp.zeros(sums.shape[1:], jnp.float32)
    kept = [jnp.sum(value, keepdims=True) for value in (dd, dc, cc)]
    for at, number in enumerate([intersection, squares, here, *kept]):
        result = jnp.where(row == at, number, result)
    sums[...] = jnp.broadcast_to(result, sums.shape)


def finish_kernel(steps, count, entries, own, image, *refs):
    earlier, gathered, (energies, kept) = refs[:steps], refs[steps : steps + count], refs[steps + count :]
    rows = [piece[device] for piece in gathered for device in range(piece.shape[0])]
    intersection = sum(row[0:1, :] for row in rows)
    squares = sum(row[1:2, :] for row in rows)
    total = intersection / squares
    kept_sq = jnp.zeros_like(total)
    for row in rows:
        shift = STEP * (total - row[2:3, :])
        kept_sq += row[3:4, :] + 2.0 * shift * row[4:5, :] + shift * shift * row[5:6, :]
    column = lax.broadcasted_iota(jnp.int32, total.shape, 1)
    listed = total
    for step, energy in enumerate(earlier):
        listed = jnp.where(column == step, energy[...], listed)
    energies[...] = listed[:, : steps + 1]
    growth = 1.0 + STEP * total
    scale = 1.0 / jnp.sqrt(jnp.maximum(kept_sq, 0.0) / entries + EPSILON)
    for t in range(image.shape[0]):
        kept[t] = ((growth * own[t] - STEP * image[t].astype(jnp.float32)) * scale).astype(jnp.bfloat16)


def local(initial_state, left_blocks, right_blocks, sources, channels, couplings, kept_rank):
    start = initial_state[0]
    left = left_blocks[0]
    right = lax.ppermute(right_blocks[0], "seg", [(0, 1), (1, 0)])
    blocks, size = start.shape[0], start.shape[1]
    width = left.shape[1]
    sectors = blocks * lax.axis_size("sec")
    entries = float(sectors * size * size)
    devices = lax.axis_size("sec")
    pairs = sources.shape[2]
    params = pltpu.CompilerParams(vmem_limit_bytes=32 * 2**20)
    ints = jax.ShapeDtypeStruct((blocks, pairs), jnp.int32)
    factors = jax.ShapeDtypeStruct((blocks, pairs), jnp.float32)
    codes, factors, left = pl.pallas_call(
        functools.partial(prepare_kernel, devices),
        out_shape=(ints, factors, jax.ShapeDtypeStruct(left.shape, left.dtype)),
        in_specs=[HBM] * 4,
        out_specs=(VMEM, VMEM, VMEM),
        scratch_shapes=[
            pltpu.VMEM(ints.shape, jnp.int32),
            pltpu.VMEM(ints.shape, jnp.int32),
            pltpu.VMEM(ints.shape, jnp.float32),
            pltpu.SemaphoreType.DMA((4,)),
        ],
        compiler_params=params,
        name="prepare",
    )(*(pltpu.with_memory_space_constraint(block, pltpu.HBM) for block in (sources[0], channels[0], couplings[0], left)))

    own_type = jax.ShapeDtypeStruct((blocks, size, size), jnp.bfloat16)
    number = jax.ShapeDtypeStruct((1, 128), jnp.float32)
    whole = (sectors, size, size)
    mixed = [pltpu.VMEM((width, size, size), jnp.bfloat16)] * blocks

    states = gather(start)
    image = pl.pallas_call(
        functools.partial(first_kernel, len(states)),
        out_shape=own_type,
        in_specs=[VMEM] * (4 + len(states)),
        out_specs=VMEM,
        scratch_shapes=[pltpu.VMEM(whole, jnp.float32), *mixed],
        compiler_params=params,
        name="first_image",
    )(codes, factors, left, right, *states)
    energies = []
    for _ in range(1, ITERS - 1):
        images = gather(image)
        energy, state, image = pl.pallas_call(
            functools.partial(middle_kernel, len(states), len(images)),
            out_shape=(number, jax.ShapeDtypeStruct(whole, jnp.float32), own_type),
            in_specs=[VMEM] * (4 + len(states) + len(images)),
            out_specs=(VMEM, VMEM, VMEM),
            scratch_shapes=mixed,
            compiler_params=params,
            name="middle_image",
        )(codes, factors, left, right, *states, *images)
        states = [state]
        energies.append(energy)
    images = gather(image)
    energy, own, image, sums = pl.pallas_call(
        functools.partial(last_kernel, len(states), len(images)),
        out_shape=(
            number,
            jax.ShapeDtypeStruct((blocks, size, size), jnp.float32),
            own_type,
            jax.ShapeDtypeStruct((1, 8, 128), jnp.float32),
        ),
        in_specs=[VMEM] * (5 + len(states) + len(images)),
        out_specs=(VMEM, VMEM, VMEM, VMEM),
        scratch_shapes=[
            pltpu.VMEM(whole, jnp.float32),
            *mixed,
        ],
        compiler_params=params,
        name="last_image",
    )(codes, factors, kept_rank, left, right, *states, *images)
    energies.append(energy)
    gathered = gather_small(sums)
    energies, kept = pl.pallas_call(
        functools.partial(finish_kernel, len(energies), len(gathered), entries),
        out_shape=(jax.ShapeDtypeStruct((1, ITERS), jnp.float32), own_type),
        in_specs=[VMEM] * (2 + len(energies) + len(gathered)),
        out_specs=(VMEM, VMEM),
        compiler_params=params,
        name="finish",
    )(own, image, *energies, *gathered)
    return kept[None], energies


def solution(mesh):
    return jax.shard_map(
        local,
        mesh=mesh,
        in_specs=(
            P(("parts", "seg"), "sec", None, None),
            P(("parts", "seg"), "sec", None, None, None),
            P(("parts", "seg"), "sec", None, None, None),
            P(("parts", "seg"), "sec", None),
            P(("parts", "seg"), "sec", None),
            P(("parts", "seg"), "sec", None),
            P(("parts", "seg"), "sec"),
        ),
        out_specs=(P(("parts", "seg"), "sec", None, None), P(("parts", "seg"), None)),
        check_vma=False,
    )
```

```python
import functools

import jax
import jax.numpy as jnp
from jax import lax
from jax.experimental import pallas as pl
from jax.experimental.pallas import tpu as pltpu
from jax.sharding import PartitionSpec as P

ITERS = 3
STEP = 0.5
EPSILON = 1e-06
SMEM = pl.BlockSpec(memory_space=pltpu.SMEM)
VMEM = pl.BlockSpec(memory_space=pltpu.VMEM)
HBM = pl.BlockSpec(memory_space=pltpu.HBM)
APART = (0, 4, 3, 2, 1, 5, 6, 7)


def hop(block, distance):
    count = lax.axis_size("sec")
    return lax.ppermute(block, "sec", [(a, a ^ distance) for a in range(count)])


def gather(block):
    if lax.axis_size("sec") != len(APART):
        return [lax.all_gather(block, "sec", axis=0, tiled=True)]
    relayed = hop(block, 4)
    near = [hop(block, distance) for distance in (3, 2, 1)]
    return [block, relayed] + near + [hop(relayed, distance) for distance in (1, 2, 3)]


def cross(block, distance):
    count = lax.axis_size("sec")
    route = [(a, count + (a ^ distance)) for a in range(count)] + [(count + a, a ^ distance) for a in range(count)]
    return lax.ppermute(block, ("seg", "sec"), route)


def gather_small(block):
    if lax.axis_size("sec") != len(APART):
        return [lax.all_gather(block, "sec", axis=0, tiled=True)]
    line = jnp.concatenate([cross(block, distance) for distance in (0, 1, 2, 3)])
    return [cross(line, 0), cross(line, 4)]


def slot(sector, blocks, devices, here):
    if devices != len(APART):
        return sector
    owner = sum((sector >= blocks * device).astype(jnp.int32) for device in range(1, devices))
    apart = owner ^ here
    place = jnp.zeros_like(sector)
    for position in range(1, devices):
        place = jnp.where(apart == APART[position], position, place)
    return place * blocks + sector - owner * blocks


def first_slot(blocks):
    return 0 if lax.axis_size("sec") == len(APART) else lax.axis_index("sec") * blocks


def code_bits(width):
    return (2 * width - 1).bit_length()


def prepare_kernel(devices, *refs):
    arguments, left, (codes, factors, near), (sources, channels, couplings, semaphores) = refs[:3], refs[3], refs[4:7], refs[7:]
    copies = fetch((*arguments, left), (sources, channels, couplings, near), semaphores)
    blocks, pairs = sources.shape
    width = near.shape[1]
    here = lax.axis_index("sec")
    down = lax.broadcasted_iota(jnp.int32, (pairs, pairs), 0)
    across = lax.broadcasted_iota(jnp.int32, (pairs, pairs), 1)

    def column(row):
        return jnp.sum(jnp.where(down == across, row, 0.0), axis=1, keepdims=True)

    for copy in copies[:3]:
        copy.wait()
    for t in range(blocks):
        channel = channels[t : t + 1, :].astype(jnp.float32)
        place = slot(sources[t : t + 1, :], blocks, devices, here).astype(jnp.float32)
        mine = column(channel)
        earlier = (channel == mine) & (across < down)
        rank = jnp.sum(jnp.where((channel < mine) | earlier, 1.0, 0.0), axis=1, keepdims=True)
        same = jnp.max(jnp.where(earlier, 1.0, 0.0), axis=1, keepdims=True)
        code = column(place) * float(1 << code_bits(width)) + 2.0 * mine + same
        chosen = rank == across.astype(jnp.float32)
        codes[t : t + 1, :] = jnp.sum(jnp.where(chosen, code, 0.0), axis=0, keepdims=True).astype(jnp.int32)
        factors[t : t + 1, :] = jnp.sum(jnp.where(chosen, column(couplings[t : t + 1, :]), 0.0), axis=0, keepdims=True)
    copies[3].wait()


def fetch(sources, targets, semaphores):
    copies = [
        pltpu.make_async_copy(source, target, semaphores.at[at])
        for at, (source, target) in enumerate(zip(sources, targets))
    ]
    for copy in copies:
        copy.start()
    return copies


def mixing(t, codes, factors, state, mixed):
    pairs = factors.shape[1]
    width, size = mixed[t].shape[0], mixed[t].shape[1]
    bits = code_bits(width)
    total = jnp.zeros((size, size), jnp.float32)
    for k in range(pairs):
        code = codes[t, k]
        term = factors[t, k] * state[lax.shift_right_logical(code, bits)]
        total = term + jnp.where((code & 1) == 1, total, 0.0)
        mixed[t][lax.shift_right_logical(code, 1) & ((1 << (bits - 1)) - 1)] = total.astype(jnp.bfloat16)


def apply_operator(codes, factors, state, left, right, mixed, image):
    blocks, width = left.shape[0], left.shape[1]
    for t in range(blocks):
        mixed[t][...] = jnp.zeros_like(mixed[t])
    for t in range(blocks):
        mixing(t, codes, factors, state, mixed)
    for t in range(blocks):
        result = jnp.zeros(image.shape[1:], jnp.float32)
        for w in range(0, width, 2):
            halves = [
                jnp.dot(left[t, v], mixed[t][v], preferred_element_type=jnp.float32).astype(jnp.bfloat16)
                for v in (w, w + 1)
            ]
            result += lax.dot_general(
                jnp.concatenate(halves, axis=1),
                jnp.concatenate([right[t, w], right[t, w + 1]], axis=1),
                (((1,), (1,)), ((), ())),
                preferred_element_type=jnp.float32,
            )
        image[t] = result.astype(jnp.bfloat16)


def spread(pieces, target):
    at = 0
    for piece in pieces:
        size = piece.shape[0]
        target[at : at + size] = piece[...].astype(jnp.float32)
        at += size


def first_kernel(count, codes, factors, left, right, *refs):
    pieces, (image, state, *mixed) = refs[:count], refs[count:]
    spread(pieces, state)
    apply_operator(codes[...], factors[...], state, left, right, mixed, image)


def rayleigh_update(before, images, after):
    shape = before[0].shape[1:]
    intersection = jnp.zeros(shape, jnp.float32)
    squares = jnp.zeros(shape, jnp.float32)
    at = 0
    flat = []
    for piece in before:
        flat += [(piece, s) for s in range(piece.shape[0])]
    pictures = []
    for piece in images:
        pictures += [(piece, s) for s in range(piece.shape[0])]
    for (piece, s), (picture, p) in zip(flat, pictures):
        value = piece[s].astype(jnp.float32)
        intersection += value * picture[p].astype(jnp.float32)
        squares += value * value
    energy = jnp.sum(intersection, keepdims=True) / jnp.sum(squares, keepdims=True)
    growth = 1.0 + STEP * energy
    for (piece, s), (picture, p) in zip(flat, pictures):
        after[at] = growth * piece[s].astype(jnp.float32) - STEP * picture[p].astype(jnp.float32)
        at += 1
    return energy


def middle_kernel(states, count, codes, factors, left, right, *refs):
    before, images = refs[:states], refs[states : states + count]
    energy, state, image, *mixed = refs[states + count :]
    energy[...] = jnp.broadcast_to(rayleigh_update(before, images, state), energy.shape)
    apply_operator(codes[...], factors[...], state, left, right, mixed, image)


def last_kernel(states, count, codes, factors, ranks, left, right, *refs):
    before, images = refs[:states], refs[states : states + count]
    energy, own, image, sums, state, *mixed = refs[states + count :]
    energy[...] = jnp.broadcast_to(rayleigh_update(before, images, state), energy.shape)
    apply_operator(codes[...], factors[...], state, left, right, mixed, image)
    blocks, size = image.shape[0], image.shape[1]
    first = first_slot(blocks)
    intersection = jnp.zeros((size, size), jnp.float32)
    squares = jnp.zeros((size, size), jnp.float32)
    for t in range(blocks):
        value = state[first + t]
        intersection += value * image[t].astype(jnp.float32)
        squares += value * value
    intersection, squares = jnp.sum(intersection, keepdims=True), jnp.sum(squares, keepdims=True)
    here = jnp.where(squares > 1e-30, intersection / jnp.maximum(squares, 1e-30), 0.0)
    growth = 1.0 + STEP * here
    column = lax.broadcasted_iota(jnp.int32, (size, size), 1)
    dd = jnp.zeros((size, size), jnp.float32)
    dc = jnp.zeros((size, size), jnp.float32)
    cc = jnp.zeros((size, size), jnp.float32)
    for t in range(blocks):
        keep = column < ranks[0:1, t : t + 1]
        value = jnp.where(keep, state[first + t], 0.0)
        picture = jnp.where(keep, image[t].astype(jnp.float32), 0.0)
        own[t] = value
        image[t] = picture.astype(jnp.bfloat16)
        moved = growth * value - STEP * picture
        dd += moved * moved
        dc += moved * value
        cc += value * value
    row = lax.broadcasted_iota(jnp.int32, sums.shape[1:], 0)
    result = jnp.zeros(sums.shape[1:], jnp.float32)
    kept = [jnp.sum(value, keepdims=True) for value in (dd, dc, cc)]
    for at, number in enumerate([intersection, squares, here, *kept]):
        result = jnp.where(row == at, number, result)
    sums[...] = jnp.broadcast_to(result, sums.shape)


def finish_kernel(steps, count, entries, own, image, *refs):
    earlier, gathered, (energies, kept) = refs[:steps], refs[steps : steps + count], refs[steps + count :]
    rows = [piece[device] for piece in gathered for device in range(piece.shape[0])]
    intersection = sum(row[0:1, :] for row in rows)
    squares = sum(row[1:2, :] for row in rows)
    total = intersection / squares
    kept_sq = jnp.zeros_like(total)
    for row in rows:
        shift = STEP * (total - row[2:3, :])
        kept_sq += row[3:4, :] + shift * (2.0 * row[4:5, :] + shift * row[5:6, :])
    column = lax.broadcasted_iota(jnp.int32, total.shape, 1)
    listed = total
    for step, energy in enumerate(earlier):
        listed = jnp.where(column == step, energy[...], listed)
    energies[...] = listed[:, : steps + 1]
    growth = 1.0 + STEP * total
    scale = 1.0 / jnp.sqrt(jnp.maximum(kept_sq, 0.0) / entries + EPSILON)
    for t in range(image.shape[0]):
        kept[t] = ((growth * own[t] - STEP * image[t].astype(jnp.float32)) * scale).astype(jnp.bfloat16)


def local(initial_state, left_blocks, right_blocks, sources, channels, couplings, kept_rank):
    start = initial_state[0]
    left = left_blocks[0]
    right = lax.ppermute(right_blocks[0], "seg", [(0, 1), (1, 0)])
    blocks, size = start.shape[0], start.shape[1]
    width = left.shape[1]
    sectors = blocks * lax.axis_size("sec")
    entries = float(sectors * size * size)
    devices = lax.axis_size("sec")
    pairs = sources.shape[2]
    params = pltpu.CompilerParams(vmem_limit_bytes=32 * 2**20)
    ints = jax.ShapeDtypeStruct((blocks, pairs), jnp.int32)
    factors = jax.ShapeDtypeStruct((blocks, pairs), jnp.float32)
    codes, factors, left = pl.pallas_call(
        functools.partial(prepare_kernel, devices),
        out_shape=(ints, factors, jax.ShapeDtypeStruct(left.shape, left.dtype)),
        in_specs=[HBM] * 4,
        out_specs=(VMEM, VMEM, VMEM),
        scratch_shapes=[
            pltpu.VMEM(ints.shape, jnp.int32),
            pltpu.VMEM(ints.shape, jnp.int32),
            pltpu.VMEM(ints.shape, jnp.float32),
            pltpu.SemaphoreType.DMA((4,)),
        ],
        compiler_params=params,
        name="prepare",
    )(*(pltpu.with_memory_space_constraint(block, pltpu.HBM) for block in (sources[0], channels[0], couplings[0], left)))

    own_type = jax.ShapeDtypeStruct((blocks, size, size), jnp.bfloat16)
    number = jax.ShapeDtypeStruct((1, 128), jnp.float32)
    whole = (sectors, size, size)
    mixed = [pltpu.VMEM((width, size, size), jnp.bfloat16)] * blocks

    states = gather(start)
    image = pl.pallas_call(
        functools.partial(first_kernel, len(states)),
        out_shape=own_type,
        in_specs=[VMEM] * (4 + len(states)),
        out_specs=VMEM,
        scratch_shapes=[pltpu.VMEM(whole, jnp.float32), *mixed],
        compiler_params=params,
        name="first_image",
    )(codes, factors, left, right, *states)
    energies = []
    for _ in range(1, ITERS - 1):
        images = gather(image)
        energy, state, image = pl.pallas_call(
            functools.partial(middle_kernel, len(states), len(images)),
            out_shape=(number, jax.ShapeDtypeStruct(whole, jnp.float32), own_type),
            in_specs=[VMEM] * (4 + len(states) + len(images)),
            out_specs=(VMEM, VMEM, VMEM),
            scratch_shapes=mixed,
            compiler_params=params,
            name="middle_image",
        )(codes, factors, left, right, *states, *images)
        states = [state]
        energies.append(energy)
    images = gather(image)
    energy, own, image, sums = pl.pallas_call(
        functools.partial(last_kernel, len(states), len(images)),
        out_shape=(
            number,
            jax.ShapeDtypeStruct((blocks, size, size), jnp.float32),
            own_type,
            jax.ShapeDtypeStruct((1, 8, 128), jnp.float32),
        ),
        in_specs=[VMEM] * (5 + len(states) + len(images)),
        out_specs=(VMEM, VMEM, VMEM, VMEM),
        scratch_shapes=[
            pltpu.VMEM(whole, jnp.float32),
            *mixed,
        ],
        compiler_params=params,
        name="last_image",
    )(codes, factors, kept_rank, left, right, *states, *images)
    energies.append(energy)
    gathered = gather_small(sums)
    energies, kept = pl.pallas_call(
        functools.partial(finish_kernel, len(energies), len(gathered), entries),
        out_shape=(jax.ShapeDtypeStruct((1, ITERS), jnp.float32), own_type),
        in_specs=[VMEM] * (2 + len(energies) + len(gathered)),
        out_specs=(VMEM, VMEM),
        compiler_params=params,
        name="finish",
    )(own, image, *energies, *gathered)
    return kept[None], energies


def solution(mesh):
    return jax.shard_map(
        local,
        mesh=mesh,
        in_specs=(
            P(("parts", "seg"), "sec", None, None),
            P(("parts", "seg"), "sec", None, None, None),
            P(("parts", "seg"), "sec", None, None, None),
            P(("parts", "seg"), "sec", None),
            P(("parts", "seg"), "sec", None),
            P(("parts", "seg"), "sec", None),
            P(("parts", "seg"), "sec"),
        ),
        out_specs=(P(("parts", "seg"), "sec", None, None), P(("parts", "seg"), None)),
        check_vma=False,
    )
```

```python
import functools

import jax
import jax.numpy as jnp
from jax import lax
from jax.experimental import pallas as pl
from jax.experimental.pallas import tpu as pltpu
from jax.sharding import PartitionSpec as P

ITERS = 3
STEP = 0.5
EPSILON = 1e-06
SMEM = pl.BlockSpec(memory_space=pltpu.SMEM)
VMEM = pl.BlockSpec(memory_space=pltpu.VMEM)
HBM = pl.BlockSpec(memory_space=pltpu.HBM)
APART = (0, 4, 3, 2, 1, 5, 6, 7)
EARLY = 5


def hop(block, distance):
    count = lax.axis_size("sec")
    return lax.ppermute(block, "sec", [(a, a ^ distance) for a in range(count)])


def gather(block):
    if lax.axis_size("sec") != len(APART):
        return [lax.all_gather(block, "sec", axis=0, tiled=True)]
    relayed = hop(block, 4)
    near = [hop(block, distance) for distance in (3, 2, 1)]
    return [block, relayed] + near + [hop(relayed, distance) for distance in (1, 2, 3)]


def cross(block, distance):
    count = lax.axis_size("sec")
    route = [(a, count + (a ^ distance)) for a in range(count)] + [(count + a, a ^ distance) for a in range(count)]
    return lax.ppermute(block, ("seg", "sec"), route)


def gather_small(block):
    if lax.axis_size("sec") != len(APART):
        return [lax.all_gather(block, "sec", axis=0, tiled=True)]
    line = jnp.concatenate([cross(block, distance) for distance in (0, 1, 2, 3)])
    return [cross(line, 0), cross(line, 4)]


def slot(sector, blocks, devices, here):
    if devices != len(APART):
        return sector
    owner = sum((sector >= blocks * device).astype(jnp.int32) for device in range(1, devices))
    apart = owner ^ here
    place = jnp.zeros_like(sector)
    for position in range(1, devices):
        place = jnp.where(apart == APART[position], position, place)
    return place * blocks + sector - owner * blocks


def first_slot(blocks):
    return 0 if lax.axis_size("sec") == len(APART) else lax.axis_index("sec") * blocks


def code_bits(width):
    return (2 * width - 1).bit_length()


def prepare_kernel(devices, *refs):
    arguments, left, (codes, factors, near), (sources, channels, couplings, semaphores) = refs[:3], refs[3], refs[4:7], refs[7:]
    copies = fetch((*arguments, left), (sources, channels, couplings, near), semaphores)
    blocks, pairs = sources.shape
    width = near.shape[1]
    here = lax.axis_index("sec")
    down = lax.broadcasted_iota(jnp.int32, (pairs, pairs), 0)
    across = lax.broadcasted_iota(jnp.int32, (pairs, pairs), 1)

    def column(row):
        return jnp.sum(jnp.where(down == across, row, 0.0), axis=1, keepdims=True)

    for copy in copies[:3]:
        copy.wait()
    for t in range(blocks):
        channel = channels[t : t + 1, :].astype(jnp.float32)
        place = slot(sources[t : t + 1, :], blocks, devices, here).astype(jnp.float32)
        mine = column(channel)
        earlier = (channel == mine) & (across < down)
        rank = jnp.sum(jnp.where((channel < mine) | earlier, 1.0, 0.0), axis=1, keepdims=True)
        same = jnp.max(jnp.where(earlier, 1.0, 0.0), axis=1, keepdims=True)
        code = column(place) * float(1 << code_bits(width)) + 2.0 * mine + same
        chosen = rank == across.astype(jnp.float32)
        codes[t : t + 1, :] = jnp.sum(jnp.where(chosen, code, 0.0), axis=0, keepdims=True).astype(jnp.int32)
        factors[t : t + 1, :] = jnp.sum(jnp.where(chosen, column(couplings[t : t + 1, :]), 0.0), axis=0, keepdims=True)
    copies[3].wait()


def fetch(sources, targets, semaphores):
    copies = [
        pltpu.make_async_copy(source, target, semaphores.at[at])
        for at, (source, target) in enumerate(zip(sources, targets))
    ]
    for copy in copies:
        copy.start()
    return copies


def mixing(t, codes, factors, state, mixed):
    pairs = factors.shape[1]
    width, size = mixed[t].shape[0], mixed[t].shape[1]
    bits = code_bits(width)
    total = jnp.zeros((size, size), jnp.float32)
    for k in range(pairs):
        code = codes[t, k]
        term = factors[t, k] * state[lax.shift_right_logical(code, bits)]
        total = term + jnp.where((code & 1) == 1, total, 0.0)
        mixed[t][lax.shift_right_logical(code, 1) & ((1 << (bits - 1)) - 1)] = total.astype(jnp.bfloat16)


def apply_operator(codes, factors, state, left, right, mixed, image):
    blocks, width = left.shape[0], left.shape[1]
    for t in range(blocks):
        mixed[t][...] = jnp.zeros_like(mixed[t])
    for t in range(blocks):
        mixing(t, codes, factors, state, mixed)
    for t in range(blocks):
        result = jnp.zeros(image.shape[1:], jnp.float32)
        for w in range(0, width, 2):
            halves = [
                jnp.dot(left[t, v], mixed[t][v], preferred_element_type=jnp.float32).astype(jnp.bfloat16)
                for v in (w, w + 1)
            ]
            result += lax.dot_general(
                jnp.concatenate(halves, axis=1),
                jnp.concatenate([right[t, w], right[t, w + 1]], axis=1),
                (((1,), (1,)), ((), ())),
                preferred_element_type=jnp.float32,
            )
        image[t] = result.astype(jnp.bfloat16)


def spread(pieces, target):
    at = 0
    for piece in pieces:
        size = piece.shape[0]
        target[at : at + size] = piece[...].astype(jnp.float32)
        at += size


def first_kernel(count, codes, factors, left, right, *refs):
    pieces, (image, state, *mixed) = refs[:count], refs[count:]
    spread(pieces, state)
    apply_operator(codes[...], factors[...], state, left, right, mixed, image)


def sector_refs(pieces):
    return [(piece, s) for piece in pieces for s in range(piece.shape[0])]


def early_kernel(states, *refs):
    before, images, sums = refs[:states], refs[states:-1], refs[-1]
    intersection = jnp.zeros(before[0].shape[1:], jnp.float32)
    squares = jnp.zeros(before[0].shape[1:], jnp.float32)
    pictures = sector_refs(images)
    for at, (piece, s) in enumerate(sector_refs(before)):
        value = piece[s].astype(jnp.float32)
        squares += value * value
        if at < len(pictures):
            picture, p = pictures[at]
            intersection += value * picture[p].astype(jnp.float32)
    for at, total in enumerate((intersection, squares)):
        sums[at] = jnp.sum(total.reshape(-1, 8, total.shape[1]), axis=0)


def rayleigh_update(before, images, early, after):
    shape = before[0].shape[1:]
    flat, pictures = sector_refs(before), sector_refs(images)
    done = len(sector_refs(images[:EARLY])) if len(images) > EARLY else 0
    intersection = jnp.zeros(shape, jnp.float32)
    squares = jnp.zeros(shape, jnp.float32)
    for at, ((piece, s), (picture, p)) in enumerate(zip(flat, pictures)):
        if at < done:
            continue
        value = piece[s].astype(jnp.float32)
        intersection += value * picture[p].astype(jnp.float32)
        if done == 0:
            squares += value * value
    if done == 0:
        energy = jnp.sum(intersection, keepdims=True) / jnp.sum(squares, keepdims=True)
    else:
        late = jnp.sum(intersection.reshape(-1, 8, shape[1]), axis=0)
        energy = jnp.sum(early[0] + late, keepdims=True) / jnp.sum(early[1], keepdims=True)
    growth = 1.0 + STEP * energy
    for at, ((piece, s), (picture, p)) in enumerate(zip(flat, pictures)):
        after[at] = growth * piece[s].astype(jnp.float32) - STEP * picture[p].astype(jnp.float32)
    return energy


def middle_kernel(states, count, early, codes, factors, left, right, *refs):
    before, images = refs[:states], refs[states : states + count]
    energy, state, image, *mixed = refs[states + count :]
    energy[...] = jnp.broadcast_to(rayleigh_update(before, images, early, state), energy.shape)
    apply_operator(codes[...], factors[...], state, left, right, mixed, image)


def last_kernel(states, count, early, codes, factors, ranks, left, right, *refs):
    before, images = refs[:states], refs[states : states + count]
    energy, own, image, sums, state, *mixed = refs[states + count :]
    energy[...] = jnp.broadcast_to(rayleigh_update(before, images, early, state), energy.shape)
    apply_operator(codes[...], factors[...], state, left, right, mixed, image)
    blocks, size = image.shape[0], image.shape[1]
    first = first_slot(blocks)
    intersection = jnp.zeros((size, size), jnp.float32)
    squares = jnp.zeros((size, size), jnp.float32)
    for t in range(blocks):
        value = state[first + t]
        intersection += value * image[t].astype(jnp.float32)
        squares += value * value
    intersection, squares = jnp.sum(intersection, keepdims=True), jnp.sum(squares, keepdims=True)
    here = jnp.where(squares > 1e-30, intersection / jnp.maximum(squares, 1e-30), 0.0)
    growth = 1.0 + STEP * here
    column = lax.broadcasted_iota(jnp.int32, (size, size), 1)
    dd = jnp.zeros((size, size), jnp.float32)
    dc = jnp.zeros((size, size), jnp.float32)
    cc = jnp.zeros((size, size), jnp.float32)
    for t in range(blocks):
        keep = column < ranks[0:1, t : t + 1]
        value = jnp.where(keep, state[first + t], 0.0)
        picture = jnp.where(keep, image[t].astype(jnp.float32), 0.0)
        own[t] = value
        image[t] = picture.astype(jnp.bfloat16)
        moved = growth * value - STEP * picture
        dd += moved * moved
        dc += moved * value
        cc += value * value
    row = lax.broadcasted_iota(jnp.int32, sums.shape[1:], 0)
    result = jnp.zeros(sums.shape[1:], jnp.float32)
    kept = [jnp.sum(value, keepdims=True) for value in (dd, dc, cc)]
    for at, number in enumerate([intersection, squares, here, *kept]):
        result = jnp.where(row == at, number, result)
    sums[...] = jnp.broadcast_to(result, sums.shape)


def finish_kernel(steps, count, entries, own, image, *refs):
    earlier, gathered, (energies, kept) = refs[:steps], refs[steps : steps + count], refs[steps + count :]
    rows = [piece[device] for piece in gathered for device in range(piece.shape[0])]
    intersection = sum(row[0:1, :] for row in rows)
    squares = sum(row[1:2, :] for row in rows)
    total = intersection / squares
    kept_sq = jnp.zeros_like(total)
    for row in rows:
        shift = STEP * (total - row[2:3, :])
        kept_sq += row[3:4, :] + shift * (2.0 * row[4:5, :] + shift * row[5:6, :])
    column = lax.broadcasted_iota(jnp.int32, total.shape, 1)
    listed = total
    for step, energy in enumerate(earlier):
        listed = jnp.where(column == step, energy[...], listed)
    energies[...] = listed[:, : steps + 1]
    growth = 1.0 + STEP * total
    scale = 1.0 / jnp.sqrt(jnp.maximum(kept_sq, 0.0) / entries + EPSILON)
    for t in range(image.shape[0]):
        kept[t] = ((growth * own[t] - STEP * image[t].astype(jnp.float32)) * scale).astype(jnp.bfloat16)


def local(initial_state, left_blocks, right_blocks, sources, channels, couplings, kept_rank):
    start = initial_state[0]
    left = left_blocks[0]
    right = lax.ppermute(right_blocks[0], "seg", [(0, 1), (1, 0)])
    blocks, size = start.shape[0], start.shape[1]
    width = left.shape[1]
    sectors = blocks * lax.axis_size("sec")
    entries = float(sectors * size * size)
    devices = lax.axis_size("sec")
    pairs = sources.shape[2]
    params = pltpu.CompilerParams(vmem_limit_bytes=32 * 2**20)
    ints = jax.ShapeDtypeStruct((blocks, pairs), jnp.int32)
    factors = jax.ShapeDtypeStruct((blocks, pairs), jnp.float32)
    codes, factors, left = pl.pallas_call(
        functools.partial(prepare_kernel, devices),
        out_shape=(ints, factors, jax.ShapeDtypeStruct(left.shape, left.dtype)),
        in_specs=[HBM] * 4,
        out_specs=(VMEM, VMEM, VMEM),
        scratch_shapes=[
            pltpu.VMEM(ints.shape, jnp.int32),
            pltpu.VMEM(ints.shape, jnp.int32),
            pltpu.VMEM(ints.shape, jnp.float32),
            pltpu.SemaphoreType.DMA((4,)),
        ],
        compiler_params=params,
        name="prepare",
    )(*(pltpu.with_memory_space_constraint(block, pltpu.HBM) for block in (sources[0], channels[0], couplings[0], left)))

    own_type = jax.ShapeDtypeStruct((blocks, size, size), jnp.bfloat16)
    number = jax.ShapeDtypeStruct((1, 128), jnp.float32)
    whole = (sectors, size, size)
    mixed = [pltpu.VMEM((width, size, size), jnp.bfloat16)] * blocks

    states = gather(start)
    image = pl.pallas_call(
        functools.partial(first_kernel, len(states)),
        out_shape=own_type,
        in_specs=[VMEM] * (4 + len(states)),
        out_specs=VMEM,
        scratch_shapes=[pltpu.VMEM(whole, jnp.float32), *mixed],
        compiler_params=params,
        name="first_image",
    )(codes, factors, left, right, *states)
    energies = []

    def early_sums(states, images):
        images = images[:EARLY] if len(images) > EARLY else images
        return pl.pallas_call(
            functools.partial(early_kernel, len(states)),
            out_shape=jax.ShapeDtypeStruct((2, 8, size), jnp.float32),
            in_specs=[VMEM] * (len(states) + len(images)),
            out_specs=VMEM,
            compiler_params=params,
            name="early_sums",
        )(*states, *images)

    for _ in range(1, ITERS - 1):
        images = gather(image)
        energy, state, image = pl.pallas_call(
            functools.partial(middle_kernel, len(states), len(images)),
            out_shape=(number, jax.ShapeDtypeStruct(whole, jnp.float32), own_type),
            in_specs=[VMEM] * (5 + len(states) + len(images)),
            out_specs=(VMEM, VMEM, VMEM),
            scratch_shapes=mixed,
            compiler_params=params,
            name="middle_image",
        )(early_sums(states, images), codes, factors, left, right, *states, *images)
        states = [state]
        energies.append(energy)
    images = gather(image)
    energy, own, image, sums = pl.pallas_call(
        functools.partial(last_kernel, len(states), len(images)),
        out_shape=(
            number,
            jax.ShapeDtypeStruct((blocks, size, size), jnp.float32),
            own_type,
            jax.ShapeDtypeStruct((1, 8, 128), jnp.float32),
        ),
        in_specs=[VMEM] * (6 + len(states) + len(images)),
        out_specs=(VMEM, VMEM, VMEM, VMEM),
        scratch_shapes=[
            pltpu.VMEM(whole, jnp.float32),
            *mixed,
        ],
        compiler_params=params,
        name="last_image",
    )(early_sums(states, images), codes, factors, kept_rank, left, right, *states, *images)
    energies.append(energy)
    gathered = gather_small(sums)
    energies, kept = pl.pallas_call(
        functools.partial(finish_kernel, len(energies), len(gathered), entries),
        out_shape=(jax.ShapeDtypeStruct((1, ITERS), jnp.float32), own_type),
        in_specs=[VMEM] * (2 + len(energies) + len(gathered)),
        out_specs=(VMEM, VMEM),
        compiler_params=params,
        name="finish",
    )(own, image, *energies, *gathered)
    return kept[None], energies


def solution(mesh):
    return jax.shard_map(
        local,
        mesh=mesh,
        in_specs=(
            P(("parts", "seg"), "sec", None, None),
            P(("parts", "seg"), "sec", None, None, None),
            P(("parts", "seg"), "sec", None, None, None),
            P(("parts", "seg"), "sec", None),
            P(("parts", "seg"), "sec", None),
            P(("parts", "seg"), "sec", None),
            P(("parts", "seg"), "sec"),
        ),
        out_specs=(P(("parts", "seg"), "sec", None, None), P(("parts", "seg"), None)),
        check_vma=False,
    )
```

```python
import functools

import jax
import jax.numpy as jnp
from jax import lax
from jax.experimental import pallas as pl
from jax.experimental.pallas import tpu as pltpu
from jax.sharding import PartitionSpec as P

ITERS = 3
STEP = 0.5
EPSILON = 1e-06
SMEM = pl.BlockSpec(memory_space=pltpu.SMEM)
VMEM = pl.BlockSpec(memory_space=pltpu.VMEM)
HBM = pl.BlockSpec(memory_space=pltpu.HBM)
APART = (0, 4, 3, 2, 1, 5, 6, 7)
EARLY = 5


def hop(block, distance):
    count = lax.axis_size("sec")
    return lax.ppermute(block, "sec", [(a, a ^ distance) for a in range(count)])


def gather(block):
    if lax.axis_size("sec") != len(APART):
        return [lax.all_gather(block, "sec", axis=0, tiled=True)]
    relayed = hop(block, 4)
    near = [hop(block, distance) for distance in (3, 2, 1)]
    return [block, relayed] + near + [hop(relayed, distance) for distance in (1, 2, 3)]


def cross(block, distance):
    count = lax.axis_size("sec")
    route = [(a, count + (a ^ distance)) for a in range(count)] + [(count + a, a ^ distance) for a in range(count)]
    return lax.ppermute(block, ("seg", "sec"), route)


def gather_small(block):
    if lax.axis_size("sec") != len(APART):
        return [lax.all_gather(block, "sec", axis=0, tiled=True)]
    line = jnp.concatenate([cross(block, distance) for distance in (0, 1, 2, 3)])
    return [cross(line, 0), cross(line, 4)]


def slot(sector, blocks, devices, here):
    if devices != len(APART):
        return sector
    owner = sum((sector >= blocks * device).astype(jnp.int32) for device in range(1, devices))
    apart = owner ^ here
    place = jnp.zeros_like(sector)
    for position in range(1, devices):
        place = jnp.where(apart == APART[position], position, place)
    return place * blocks + sector - owner * blocks


def first_slot(blocks):
    return 0 if lax.axis_size("sec") == len(APART) else lax.axis_index("sec") * blocks


def code_bits(width):
    return (2 * width - 1).bit_length()


def prepare_kernel(devices, *refs):
    arguments, left, (codes, factors, near), (sources, channels, couplings, semaphores) = refs[:3], refs[3], refs[4:7], refs[7:]
    copies = fetch((*arguments, left), (sources, channels, couplings, near), semaphores)
    blocks, pairs = sources.shape
    width = near.shape[1]
    here = lax.axis_index("sec")
    down = lax.broadcasted_iota(jnp.int32, (pairs, pairs), 0)
    across = lax.broadcasted_iota(jnp.int32, (pairs, pairs), 1)

    def column(row):
        return jnp.sum(jnp.where(down == across, row, 0.0), axis=1, keepdims=True)

    for copy in copies[:3]:
        copy.wait()
    for t in range(blocks):
        channel = channels[t : t + 1, :].astype(jnp.float32)
        place = slot(sources[t : t + 1, :], blocks, devices, here).astype(jnp.float32)
        mine = column(channel)
        earlier = (channel == mine) & (across < down)
        rank = jnp.sum(jnp.where((channel < mine) | earlier, 1.0, 0.0), axis=1, keepdims=True)
        same = jnp.max(jnp.where(earlier, 1.0, 0.0), axis=1, keepdims=True)
        code = column(place) * float(1 << code_bits(width)) + 2.0 * mine + same
        chosen = rank == across.astype(jnp.float32)
        codes[t : t + 1, :] = jnp.sum(jnp.where(chosen, code, 0.0), axis=0, keepdims=True).astype(jnp.int32)
        factors[t : t + 1, :] = jnp.sum(jnp.where(chosen, column(couplings[t : t + 1, :]), 0.0), axis=0, keepdims=True)
    copies[3].wait()


def fetch(sources, targets, semaphores):
    copies = [
        pltpu.make_async_copy(source, target, semaphores.at[at])
        for at, (source, target) in enumerate(zip(sources, targets))
    ]
    for copy in copies:
        copy.start()
    return copies


def mixing(t, codes, factors, state, mixed):
    pairs = factors.shape[1]
    width, size = mixed[t].shape[0], mixed[t].shape[1]
    bits = code_bits(width)
    total = jnp.zeros((size, size), jnp.float32)
    for k in range(pairs):
        code = codes[t, k]
        term = factors[t, k] * state[lax.shift_right_logical(code, bits)]
        total = term + jnp.where((code & 1) == 1, total, 0.0)
        mixed[t][lax.shift_right_logical(code, 1) & ((1 << (bits - 1)) - 1)] = total.astype(jnp.bfloat16)


def apply_operator(codes, factors, state, left, right, mixed, image):
    blocks, width = left.shape[0], left.shape[1]
    nothing = jnp.zeros(image.shape[1:], jnp.bfloat16)
    for t in range(blocks):
        mixed[t][...] = jnp.zeros_like(mixed[t])
    for t in range(blocks):
        mixing(t, codes, factors, state, mixed)
    for t in range(blocks):
        result = jnp.zeros(image.shape[1:], jnp.float32)
        for w in range(0, width, 2):
            pair = jnp.concatenate([left[t, w], left[t, w + 1]], axis=1)
            apart = jnp.concatenate(
                [
                    jnp.concatenate([mixed[t][w], nothing], axis=1),
                    jnp.concatenate([nothing, mixed[t][w + 1]], axis=1),
                ],
                axis=0,
            )
            result += lax.dot_general(
                jnp.dot(pair, apart, preferred_element_type=jnp.float32).astype(jnp.bfloat16),
                jnp.concatenate([right[t, w], right[t, w + 1]], axis=1),
                (((1,), (1,)), ((), ())),
                preferred_element_type=jnp.float32,
            )
        image[t] = result.astype(jnp.bfloat16)


def spread(pieces, target):
    at = 0
    for piece in pieces:
        size = piece.shape[0]
        target[at : at + size] = piece[...].astype(jnp.float32)
        at += size


def first_kernel(count, codes, factors, left, right, *refs):
    pieces, (image, state, *mixed) = refs[:count], refs[count:]
    spread(pieces, state)
    apply_operator(codes[...], factors[...], state, left, right, mixed, image)


def sector_refs(pieces):
    return [(piece, s) for piece in pieces for s in range(piece.shape[0])]


def early_kernel(states, *refs):
    before, images, sums = refs[:states], refs[states:-1], refs[-1]
    intersection = jnp.zeros(before[0].shape[1:], jnp.float32)
    squares = jnp.zeros(before[0].shape[1:], jnp.float32)
    pictures = sector_refs(images)
    for at, (piece, s) in enumerate(sector_refs(before)):
        value = piece[s].astype(jnp.float32)
        squares += value * value
        if at < len(pictures):
            picture, p = pictures[at]
            intersection += value * picture[p].astype(jnp.float32)
    for at, total in enumerate((intersection, squares)):
        sums[at] = jnp.sum(total.reshape(-1, 8, total.shape[1]), axis=0)


def rayleigh_update(before, images, early, after):
    shape = before[0].shape[1:]
    flat, pictures = sector_refs(before), sector_refs(images)
    done = len(sector_refs(images[:EARLY])) if len(images) > EARLY else 0
    intersection = jnp.zeros(shape, jnp.float32)
    squares = jnp.zeros(shape, jnp.float32)
    for at, ((piece, s), (picture, p)) in enumerate(zip(flat, pictures)):
        if at < done:
            continue
        value = piece[s].astype(jnp.float32)
        intersection += value * picture[p].astype(jnp.float32)
        if done == 0:
            squares += value * value
    if done == 0:
        energy = jnp.sum(intersection, keepdims=True) / jnp.sum(squares, keepdims=True)
    else:
        late = jnp.sum(intersection.reshape(-1, 8, shape[1]), axis=0)
        energy = jnp.sum(early[0] + late, keepdims=True) / jnp.sum(early[1], keepdims=True)
    growth = 1.0 + STEP * energy
    for at, ((piece, s), (picture, p)) in enumerate(zip(flat, pictures)):
        after[at] = growth * piece[s].astype(jnp.float32) - STEP * picture[p].astype(jnp.float32)
    return energy


def middle_kernel(states, count, early, codes, factors, left, right, *refs):
    before, images = refs[:states], refs[states : states + count]
    energy, state, image, *mixed = refs[states + count :]
    energy[...] = jnp.broadcast_to(rayleigh_update(before, images, early, state), energy.shape)
    apply_operator(codes[...], factors[...], state, left, right, mixed, image)


def last_kernel(states, count, early, codes, factors, ranks, left, right, *refs):
    before, images = refs[:states], refs[states : states + count]
    energy, own, image, sums, state, *mixed = refs[states + count :]
    energy[...] = jnp.broadcast_to(rayleigh_update(before, images, early, state), energy.shape)
    apply_operator(codes[...], factors[...], state, left, right, mixed, image)
    blocks, size = image.shape[0], image.shape[1]
    first = first_slot(blocks)
    intersection = jnp.zeros((size, size), jnp.float32)
    squares = jnp.zeros((size, size), jnp.float32)
    for t in range(blocks):
        value = state[first + t]
        intersection += value * image[t].astype(jnp.float32)
        squares += value * value
    intersection, squares = jnp.sum(intersection, keepdims=True), jnp.sum(squares, keepdims=True)
    here = jnp.where(squares > 1e-30, intersection / jnp.maximum(squares, 1e-30), 0.0)
    growth = 1.0 + STEP * here
    column = lax.broadcasted_iota(jnp.int32, (size, size), 1)
    dd = jnp.zeros((size, size), jnp.float32)
    dc = jnp.zeros((size, size), jnp.float32)
    cc = jnp.zeros((size, size), jnp.float32)
    for t in range(blocks):
        keep = column < ranks[0:1, t : t + 1]
        value = jnp.where(keep, state[first + t], 0.0)
        picture = jnp.where(keep, image[t].astype(jnp.float32), 0.0)
        own[t] = value
        image[t] = picture.astype(jnp.bfloat16)
        moved = growth * value - STEP * picture
        dd += moved * moved
        dc += moved * value
        cc += value * value
    row = lax.broadcasted_iota(jnp.int32, sums.shape[1:], 0)
    result = jnp.zeros(sums.shape[1:], jnp.float32)
    kept = [jnp.sum(value, keepdims=True) for value in (dd, dc, cc)]
    for at, number in enumerate([intersection, squares, here, *kept]):
        result = jnp.where(row == at, number, result)
    sums[...] = jnp.broadcast_to(result, sums.shape)


def finish_kernel(steps, count, entries, own, image, *refs):
    earlier, gathered, (energies, kept) = refs[:steps], refs[steps : steps + count], refs[steps + count :]
    rows = [piece[device] for piece in gathered for device in range(piece.shape[0])]
    intersection = sum(row[0:1, :] for row in rows)
    squares = sum(row[1:2, :] for row in rows)
    total = intersection / squares
    kept_sq = jnp.zeros_like(total)
    for row in rows:
        shift = STEP * (total - row[2:3, :])
        kept_sq += row[3:4, :] + shift * (2.0 * row[4:5, :] + shift * row[5:6, :])
    column = lax.broadcasted_iota(jnp.int32, total.shape, 1)
    listed = total
    for step, energy in enumerate(earlier):
        listed = jnp.where(column == step, energy[...], listed)
    energies[...] = listed[:, : steps + 1]
    growth = 1.0 + STEP * total
    scale = 1.0 / jnp.sqrt(jnp.maximum(kept_sq, 0.0) / entries + EPSILON)
    for t in range(image.shape[0]):
        kept[t] = ((growth * own[t] - STEP * image[t].astype(jnp.float32)) * scale).astype(jnp.bfloat16)


def local(initial_state, left_blocks, right_blocks, sources, channels, couplings, kept_rank):
    start = initial_state[0]
    left = left_blocks[0]
    right = lax.ppermute(right_blocks[0], "seg", [(0, 1), (1, 0)])
    blocks, size = start.shape[0], start.shape[1]
    width = left.shape[1]
    sectors = blocks * lax.axis_size("sec")
    entries = float(sectors * size * size)
    devices = lax.axis_size("sec")
    pairs = sources.shape[2]
    params = pltpu.CompilerParams(vmem_limit_bytes=32 * 2**20)
    ints = jax.ShapeDtypeStruct((blocks, pairs), jnp.int32)
    factors = jax.ShapeDtypeStruct((blocks, pairs), jnp.float32)
    codes, factors, left = pl.pallas_call(
        functools.partial(prepare_kernel, devices),
        out_shape=(ints, factors, jax.ShapeDtypeStruct(left.shape, left.dtype)),
        in_specs=[HBM] * 4,
        out_specs=(VMEM, VMEM, VMEM),
        scratch_shapes=[
            pltpu.VMEM(ints.shape, jnp.int32),
            pltpu.VMEM(ints.shape, jnp.int32),
            pltpu.VMEM(ints.shape, jnp.float32),
            pltpu.SemaphoreType.DMA((4,)),
        ],
        compiler_params=params,
        name="prepare",
    )(*(pltpu.with_memory_space_constraint(block, pltpu.HBM) for block in (sources[0], channels[0], couplings[0], left)))

    own_type = jax.ShapeDtypeStruct((blocks, size, size), jnp.bfloat16)
    number = jax.ShapeDtypeStruct((1, 128), jnp.float32)
    whole = (sectors, size, size)
    mixed = [pltpu.VMEM((width, size, size), jnp.bfloat16)] * blocks

    states = gather(start)
    image = pl.pallas_call(
        functools.partial(first_kernel, len(states)),
        out_shape=own_type,
        in_specs=[VMEM] * (4 + len(states)),
        out_specs=VMEM,
        scratch_shapes=[pltpu.VMEM(whole, jnp.float32), *mixed],
        compiler_params=params,
        name="first_image",
    )(codes, factors, left, right, *states)
    energies = []

    def early_sums(states, images):
        images = images[:EARLY] if len(images) > EARLY else images
        return pl.pallas_call(
            functools.partial(early_kernel, len(states)),
            out_shape=jax.ShapeDtypeStruct((2, 8, size), jnp.float32),
            in_specs=[VMEM] * (len(states) + len(images)),
            out_specs=VMEM,
            compiler_params=params,
            name="early_sums",
        )(*states, *images)

    for _ in range(1, ITERS - 1):
        images = gather(image)
        energy, state, image = pl.pallas_call(
            functools.partial(middle_kernel, len(states), len(images)),
            out_shape=(number, jax.ShapeDtypeStruct(whole, jnp.float32), own_type),
            in_specs=[VMEM] * (5 + len(states) + len(images)),
            out_specs=(VMEM, VMEM, VMEM),
            scratch_shapes=mixed,
            compiler_params=params,
            name="middle_image",
        )(early_sums(states, images), codes, factors, left, right, *states, *images)
        states = [state]
        energies.append(energy)
    images = gather(image)
    energy, own, image, sums = pl.pallas_call(
        functools.partial(last_kernel, len(states), len(images)),
        out_shape=(
            number,
            jax.ShapeDtypeStruct((blocks, size, size), jnp.float32),
            own_type,
            jax.ShapeDtypeStruct((1, 8, 128), jnp.float32),
        ),
        in_specs=[VMEM] * (6 + len(states) + len(images)),
        out_specs=(VMEM, VMEM, VMEM, VMEM),
        scratch_shapes=[
            pltpu.VMEM(whole, jnp.float32),
            *mixed,
        ],
        compiler_params=params,
        name="last_image",
    )(early_sums(states, images), codes, factors, kept_rank, left, right, *states, *images)
    energies.append(energy)
    gathered = gather_small(sums)
    energies, kept = pl.pallas_call(
        functools.partial(finish_kernel, len(energies), len(gathered), entries),
        out_shape=(jax.ShapeDtypeStruct((1, ITERS), jnp.float32), own_type),
        in_specs=[VMEM] * (2 + len(energies) + len(gathered)),
        out_specs=(VMEM, VMEM),
        compiler_params=params,
        name="finish",
    )(own, image, *energies, *gathered)
    return kept[None], energies


def solution(mesh):
    return jax.shard_map(
        local,
        mesh=mesh,
        in_specs=(
            P(("parts", "seg"), "sec", None, None),
            P(("parts", "seg"), "sec", None, None, None),
            P(("parts", "seg"), "sec", None, None, None),
            P(("parts", "seg"), "sec", None),
            P(("parts", "seg"), "sec", None),
            P(("parts", "seg"), "sec", None),
            P(("parts", "seg"), "sec"),
        ),
        out_specs=(P(("parts", "seg"), "sec", None, None), P(("parts", "seg"), None)),
        check_vma=False,
    )
```
